256 devices in a mesh: row: 8 (over z), col: 32 (over x, y, core).
Axes of the slice: x: 4, y: 4, z: 8, core: 2. Of those that a mesh axis runs over, the one named last changes fastest.
Arguments:
- frontal: float32 [8192, 65536], P('row', 'col'), may hold values from -6 to 6
- sketch: float32 [65536, 256], P('col'), may hold values from -0.0234375 to 0.0234375
- rank_table: int32 [3, 8], replicated, may hold values from 64 to 256, as said below
Outputs:
- leaf_basis: float32 [8192, 256], P(('row', 'col'))
- top_basis: float32 [8192, 256], P(('row', 'col'))
- coupling: float32 [2048, 65536], P('row', 'col')
The draws below stay inside these ranges and needn't reach their ends.
Inputs may be any that keep to these rules, and one draw needn't show every extreme that they name: rank_table[l, g] is the rank of the level-l node made of the 2**l consecutive row groups holding g, equal over the groups of that node; a node's rank is at most the larger of its two children's ranks; in every draw some leaf has rank 256 and some leaf rank 256 // 4.
All inputs are finite; a program needn't handle non-finite values.
Results may differ from the reference program's by a relative error of at most 0.00012.
Values sent between devices are 32-bit elements; how exact they have to be, the bound alone decides.
A program may use at most 64 MiB of HBM per device.

```python
import jax
import jax.numpy as jnp
from jax import lax

S = 256
LEVELS = 2
ROWS = 8192
COLS = 65536
N_ROW = 8


def draw_rank_table(key, part):
    lowest = S // 4
    leaf_key = jax.random.fold_in(key, 11)
    perm_key = jax.random.fold_in(key, 23)
    leaves = jax.random.randint(leaf_key, (N_ROW,), lowest, S + 1)
    order = jax.random.permutation(perm_key, N_ROW)
    leaves = leaves.at[order[0]].set(S)
    leaves = leaves.at[order[1]].set(lowest)
    leaves = leaves.astype(jnp.int32)
    rows_list = [leaves]
    previous = leaves
    for height in range(1, LEVELS + 1):
        node_span = 2 ** height
        child_ranks = previous.reshape(N_ROW // node_span, 2, node_span // 2)[:, :, 0]
        largest = jnp.max(child_ranks, axis=1)
        node_key = jax.random.fold_in(key, 100 + height)
        spread = jax.random.randint(node_key, (N_ROW // node_span,), 0, largest - lowest + 1)
        node_ranks = (lowest + spread).astype(jnp.int32)
        previous = jnp.repeat(node_ranks, node_span)
        rows_list.append(previous)
    return jnp.stack(rows_list, axis=0).astype(jnp.int32)


def strengthened(values, stream_key, source, target, shards_of, factor):
    def block_of(dim):
        return (jnp.arange(values.shape[dim]) // (values.shape[dim] // shards_of)).reshape((-1,) + (1,) * (values.ndim - 1 - dim))

    one_side = jax.random.permutation(stream_key, shards_of)[block_of(target)]
    second = (block_of(target) + shards_of // 2) % shards_of
    return jnp.where((block_of(source) == one_side) | (block_of(source) == second), factor * values, values)


def block_levels(stream_key, extent, pieces, least, top_value):
    loudness = 1.0
    for axis_at, shards_of in pieces:
        draws = jax.random.uniform(jax.random.fold_in(jax.random.fold_in(stream_key, 6), axis_at), (shards_of,), jnp.float32, least / len(pieces), top_value / len(pieces))
        loudness = loudness * jnp.repeat(jnp.exp(draws), extent[axis_at] // shards_of).reshape((-1,) + (1,) * (len(extent) - 1 - axis_at))
    return loudness


def normal_values(rng, extent, deviation, limit, split=(), kind=jnp.bfloat16):
    factor_of = block_levels(rng, extent, split, -0.22, 0.18) if split else 1.0
    drawn = jax.random.normal(rng, extent, jnp.float32) * deviation * factor_of
    return jnp.minimum(jnp.maximum(drawn, -limit), limit).astype(kind)


def heavy_noise(key, dims, scale, most, cuts, heavy, held_as=jnp.bfloat16):
    values = scale * jax.random.normal(key, dims, jnp.float32)
    if cuts:
        values = values * block_levels(key, dims, cuts, -0.22, 0.18)
    return jnp.clip(strengthened(values, jax.random.fold_in(key, 3), *heavy), -most, most).astype(held_as)


def setup_inputs(seed: int = 0) -> dict:
    key_of = jax.random.split(jax.random.key(seed), 4)
    return {
        "frontal": heavy_noise(key_of[0], (ROWS, COLS), 1.0, 6.0, ((0, 8), (1, 32)), (1, 0, 32, 2.75), jnp.float32),
        "sketch": normal_values(key_of[1], (COLS, S), COLS ** -0.5, 0.0234375, ((0, 32),), jnp.float32),
        "rank_table": draw_rank_table(jax.random.fold_in(key_of[3], 71), 0),
    }


def product(left, right):
    return jnp.dot(left.astype(jnp.float32), right.astype(jnp.float32), precision=lax.Precision.HIGHEST, preferred_element_type=jnp.float32)

def mask_of(rank_value, width):
    return (jnp.arange(width) < rank_value).astype(jnp.float32)

def factor(gram_full, keep_mask):
    masked = keep_mask[:, None] * gram_full * keep_mask[None, :] + jnp.diag(1.0 - keep_mask)
    return jnp.linalg.cholesky(masked)

def right_solve(factor_low, operand):
    return lax.linalg.triangular_solve(factor_low, operand, left_side=False, lower=True, transpose_a=True)

def left_solve(factor_low, operand):
    return lax.linalg.triangular_solve(factor_low, operand, left_side=True, lower=True)

def reference(frontal, sketch, rank_table):
    width = sketch.shape[1]
    groups = rank_table.shape[1]
    row_count = frontal.shape[0] // groups
    bases = []
    coords = []
    couplings = []
    for member in range(groups):
        row_block = frontal[member * row_count:(member + 1) * row_count]
        samples = product(row_block, sketch)
        gram_full = product(samples.T, samples)
        keep_mask = mask_of(rank_table[0, member], width)
        factor_low = factor(gram_full, keep_mask)
        leaf_basis = right_solve(factor_low, samples * keep_mask[None, :])
        bases.append(leaf_basis)
        coords.append(left_solve(factor_low, keep_mask[:, None] * gram_full))
        couplings.append(product(leaf_basis.T, row_block))
    chains = [jnp.eye(width, dtype=jnp.float32) for member in range(groups)]
    for height in range(1, LEVELS + 1):
        node_span = 2 ** height
        half_span = node_span // 2
        for first_group in range(0, groups, node_span):
            coords_low = coords[first_group]
            coords_high = coords[first_group + half_span]
            pair_gram = product(coords_low.T, coords_low) + product(coords_high.T, coords_high)
            node_mask = mask_of(rank_table[height, first_group], width)
            factor_low = factor(pair_gram, node_mask)
            transfer_low = right_solve(factor_low, coords_low * node_mask[None, :])
            transfer_high = right_solve(factor_low, coords_high * node_mask[None, :])
            parent_coords = left_solve(factor_low, node_mask[:, None] * pair_gram)
            for member in range(first_group, first_group + node_span):
                if member < first_group + half_span:
                    chains[member] = product(chains[member], transfer_low)
                else:
                    chains[member] = product(chains[member], transfer_high)
                coords[member] = parent_coords
    leaf_basis = jnp.concatenate(bases, axis=0)
    top_basis = jnp.concatenate([product(bases[member], chains[member]) for member in range(groups)], axis=0)
    coupling = jnp.concatenate(couplings, axis=0)
    return (leaf_basis, top_basis, coupling)
```

```python
import functools

import jax
import jax.numpy as jnp
from jax import lax
from jax.experimental import pallas as pl
from jax.experimental.pallas import tpu as pltpu
from jax.sharding import PartitionSpec as P

MESH = pl.DeviceIdType.MESH
NN = (((1,), (0,)), ((), ()))
NT = (((1,), (1,)), ((), ()))
TN = (((0,), (0,)), ((), ()))
PB = 32
F32 = jnp.float32


def split(x):
    hi = x.astype(jnp.bfloat16)
    return hi, (x - hi.astype(F32)).astype(jnp.bfloat16)


def dot3(a, b, dims=NN):
    ah, al = a if isinstance(a, tuple) else split(a)
    bh, bl = b if isinstance(b, tuple) else split(b)
    d = functools.partial(lax.dot_general, dimension_numbers=dims, preferred_element_type=F32)
    return d(ah, bh) + (d(ah, bl) + d(al, bh))


def diag_inverse(x):
    lane = lax.broadcasted_iota(jnp.int32, (8, 128), 1)
    sub = lax.broadcasted_iota(jnp.int32, (8, 128), 0)
    base = (lane // PB) * PB
    n = [jnp.where(lane % PB == sub + 8 * g, 1.0, 0.0).astype(jnp.float32) for g in range(4)]
    m = list(x)
    scale = [jnp.zeros((8, 128), jnp.float32) for _ in range(4)]
    for q in range(4):
        c = {}
        for k in range(8):
            for g in range(q, 4):
                c[k, g] = jnp.take_along_axis(m[g], base + (8 * q + k), axis=1)
        for j in range(8):
            def row(v):
                return jnp.broadcast_to(v[j:j + 1, :], (8, 128))
            p = row(c[j, q])
            rs = lax.rsqrt(p)
            r = rs * rs
            scale[q] = jnp.where(sub == j, rs, scale[q])
            crow = {k: row(c[k, q]) for k in range(j + 1, 8)}
            mrow = row(m[q]) if q < 3 else None
            nrow = row(n[q])
            for g in range(q, 4):
                f = c[j, g] * r
                if g == q:
                    f = jnp.where(sub > j, f, 0.0)
                for k in range(j + 1, 8):
                    c[k, g] = c[k, g] - f * crow[k]
                if q < 3:
                    m[g] = m[g] - f * mrow
                n[g] = n[g] - f * nrow
    return [n[g] * scale[g] for g in range(4)]

def chol_inverse(z_ref, batch, count=256):
    def tile_step(t, _):
        lane0 = pl.multiple_of(t * 128, 128)
        for s in range(128 // PB):
            start = pl.multiple_of(t * 128 + s * PB, PB)
            lane = lax.broadcasted_iota(jnp.int32, (8, 128), 1)
            packed = []
            for g in range(4):
                v = None
                for b in range(4):
                    bb = b if b < batch else 0
                    d = z_ref[bb, pl.ds(start + 8 * g, 8), pl.ds(lane0, 128)]
                    shift = (PB * b - PB * s) % 128
                    if shift:
                        d = pltpu.roll(d, shift, 1)
                    v = d if v is None else jnp.where(lane // PB == b, d, v)
                packed.append(v)
            w4 = jnp.concatenate(diag_inverse(packed), axis=0)
            rows = lax.broadcasted_iota(jnp.int32, (256, 1), 0)
            lanes = lax.broadcasted_iota(jnp.int32, (1, 256), 1)
            incol = (lanes >= start) & (lanes < start + PB)
            eye = (lax.broadcasted_iota(jnp.int32, (PB, 256), 1) == lax.broadcasted_iota(jnp.int32, (PB, 256), 0) + start)
            for b in range(batch):
                w = split(w4[:, PB * b:PB * (b + 1)])
                r = z_ref[b, pl.ds(start, PB), :]
                r = jnp.where(incol, eye.astype(jnp.float32), r)
                u = dot3(w, split(r))
                zc = z_ref[b, :, pl.ds(lane0, 128)][:, PB * s:PB * (s + 1)]
                lm = dot3(split(zc), w, NT)
                lm = jnp.where(rows >= start + PB, lm, 0.0)
                z = z_ref[b]
                z = jnp.where(incol & (rows >= start), 0.0, z)
                z_ref[b] = z - dot3(split(lm), split(u))
                z_ref[b, pl.ds(start, PB), :] = u
        return 0
    lax.fori_loop(0, 2, tile_step, 0)
    r = lax.broadcasted_iota(jnp.int32, (256, 256), 0)
    cc = lax.broadcasted_iota(jnp.int32, (256, 256), 1)
    for b in range(batch):
        z_ref[b] = jnp.where(cc <= r, z_ref[b], 0.0)

def gather_kernel(f_hbm, s_hbm, samples, grams, fbuf, sbuf, sh, sl, part, xbuf, outbuf, rbuf, acc,
                  fsem, ssem, xs_sem, xr_sem, rs_sem, rr_sem, as_sem, ar_sem, ws_sem, wr_sem,
                  zs_sem, zr_sem, gs_sem, gr_sem, hs_sem, hr_sem):
    z = lax.axis_index("row")
    me = lax.axis_index("col")
    core = lax.rem(me, 2)
    chip = lax.div(me, 2)
    x = lax.div(chip, 4)
    y = lax.rem(chip, 4)
    quad = lax.div(z, 4) * 4
    zq = lax.rem(z, 4)
    sibling = {"row": z, "col": chip * 2 + 1 - core}

    def peer(q):
        return {"row": z, "col": q * 2 + core}

    def along_z(m):
        return {"row": quad + m, "col": me}

    def chunk_copy(s):
        rows = pl.multiple_of(lax.rem(x + 1 + s, 4) * 256, 256)
        return pltpu.make_async_copy(f_hbm.at[pl.ds(rows, 256)], fbuf.at[s], fsem.at[s])

    scopy = pltpu.make_async_copy(s_hbm, sbuf, ssem)
    scopy.start()
    for s in range(4):
        chunk_copy(s).start()

    barrier = pltpu.get_barrier_semaphore()
    pl.semaphore_signal(barrier, inc=1, device_id=sibling, device_id_type=MESH)

    @pl.loop(1, 16)
    def _(t):
        pl.semaphore_signal(barrier, inc=1, device_id=peer(lax.rem(chip + t, 16)), device_id_type=MESH)

    for t in range(1, 4):
        pl.semaphore_signal(barrier, inc=1, device_id=along_z(lax.rem(zq + t, 4)), device_id_type=MESH)

    scopy.wait()
    sh[...], sl[...] = split(sbuf[...])
    pl.semaphore_wait(barrier, 19)

    def remote(src, dst, send, recv, device):
        return pltpu.make_async_remote_copy(src_ref=src, dst_ref=dst, send_sem=send, recv_sem=recv,
                                            device_id=device, device_id_type=MESH)

    def cores_copy(s):
        return remote(part.at[s, :, 1 - core], xbuf.at[s], xs_sem.at[s], xr_sem.at[s], sibling)

    def shard_copy(s, yy, q):
        return remote(outbuf.at[s, yy], rbuf.at[chip], rs_sem.at[q], rr_sem.at[chip], peer(q))

    @pl.loop(0, 5)
    def _(s):
        @pl.when(s < 4)
        def _():
            chunk_copy(s).wait()
            p = dot3(split(fbuf[s]), (sh[...], sl[...]))
            part[s] = p.reshape(4, 2, 32, 256)
            cores_copy(s).start()

        @pl.when(s > 0)
        def _():
            t = s - 1
            xt = lax.rem(x + 1 + t, 4)
            cores_copy(t).wait_recv()
            outbuf[t] = part[t, :, core] + xbuf[t]

            @pl.loop(0, 4)
            def _(u):
                yy = lax.rem(y + 1 + u, 4)
                q = xt * 4 + yy

                @pl.when(q != chip)
                def _():
                    shard_copy(t, yy, q).start()

    acc[...] = outbuf[3, y]

    @pl.loop(1, 16)
    def _(t):
        q = lax.rem(chip + t, 16)
        remote(outbuf.at[0, 0], rbuf.at[q], rs_sem.at[q], rr_sem.at[q], peer(q)).wait_recv()
        acc[...] += rbuf[q]

    samples[me] = acc[...]

    def own_copy(q):
        return remote(samples.at[me], samples.at[me], as_sem.at[q], ar_sem.at[chip], peer(q))

    def relay_copy(q):
        return remote(samples.at[q * 2 + core], samples.at[q * 2 + core], ws_sem.at[q], wr_sem.at[q], sibling)

    @pl.loop(1, 16)
    def _(t):
        own_copy(lax.rem(chip + t, 16)).start()

    relay_copy(chip).start()

    @pl.loop(1, 16)
    def _(t):
        q = lax.rem(chip + 16 - t, 16)
        remote(samples.at[me], samples.at[q * 2 + core], as_sem.at[q], ar_sem.at[q], peer(q)).wait_recv()
        relay_copy(q).start()

    @pl.loop(0, 16)
    def _(q):
        remote(samples.at[q * 2 + core], samples.at[q * 2 + 1 - core], ws_sem.at[q], wr_sem.at[q], sibling).wait_recv()

    full = split(samples[...].reshape(1024, 256))
    grams[0] = dot3(full, full, TN).reshape(32, 8, 256)

    def z_copy(t):
        return remote(grams.at[0, me], grams.at[t, me], zs_sem.at[t], zr_sem.at[t], along_z(lax.rem(zq + 4 - t, 4)))

    for t in range(1, 4):
        z_copy(t).start()
    for t in range(1, 4):
        z_copy(t).wait_recv()

    def gram_slice(c):
        return grams.at[pl.ds(1, 3), c]

    def gram_copy(q):
        return remote(gram_slice(me), gram_slice(me), gs_sem.at[q], gr_sem.at[chip], peer(q))

    def gram_relay(q):
        return remote(gram_slice(q * 2 + core), gram_slice(q * 2 + core), hs_sem.at[q], hr_sem.at[q], sibling)

    @pl.loop(1, 16)
    def _(t):
        gram_copy(lax.rem(chip + t, 16)).start()

    gram_relay(chip).start()

    @pl.loop(1, 16)
    def _(t):
        q = lax.rem(chip + 16 - t, 16)
        remote(gram_slice(me), gram_slice(q * 2 + core), gs_sem.at[q], gr_sem.at[q], peer(q)).wait_recv()
        gram_relay(q).start()

    @pl.loop(0, 16)
    def _(q):
        remote(gram_slice(q * 2 + core), gram_slice(q * 2 + 1 - core), hs_sem.at[q], hr_sem.at[q], sibling).wait_recv()

    for s in range(4):
        cores_copy(s).wait_send()
    for t in range(1, 4):
        z_copy(t).wait_send()

    @pl.loop(1, 16)
    def _(t):
        q = lax.rem(chip + t, 16)
        shard_copy(0, 0, q).wait_send()
        own_copy(q).wait_send()
        gram_copy(q).wait_send()

    @pl.loop(0, 16)
    def _(q):
        relay_copy(q).wait_send()
        gram_relay(q).wait_send()


def gathered(frontal, sketch):
    vmem = pl.BlockSpec(memory_space=pltpu.VMEM)
    hbm = pl.BlockSpec(memory_space=pl.ANY)
    dma = pltpu.SemaphoreType.DMA
    return pl.pallas_call(
        gather_kernel,
        out_shape=(jax.ShapeDtypeStruct((32, 32, 256), F32), jax.ShapeDtypeStruct((4, 32, 8, 256), F32)),
        in_specs=[hbm, hbm],
        out_specs=(vmem, vmem),
        scratch_shapes=[
            pltpu.VMEM((4, 256, 2048), F32),
            pltpu.VMEM((2048, 256), F32),
            pltpu.VMEM((2048, 256), jnp.bfloat16),
            pltpu.VMEM((2048, 256), jnp.bfloat16),
            pltpu.VMEM((4, 4, 2, 32, 256), F32),
            pltpu.VMEM((4, 4, 32, 256), F32),
            pltpu.VMEM((4, 4, 32, 256), F32),
            pltpu.VMEM((16, 32, 256), F32),
            pltpu.VMEM((32, 256), F32),
            dma((4,)), dma, dma((4,)), dma((4,)),
            dma((16,)), dma((16,)), dma((16,)), dma((16,)), dma((16,)), dma((16,)),
            dma((4,)), dma((4,)), dma((16,)), dma((16,)), dma((16,)), dma((16,)),
        ],
        compiler_params=pltpu.CompilerParams(collective_id=0, has_side_effects=True, vmem_limit_bytes=40 * 2**20),
        cost_estimate=pl.CostEstimate(flops=3 * 2**30, bytes_accessed=10 * 2**20, transcendentals=0),
    )(frontal, sketch)


def masked(gram, rank):
    r = lax.broadcasted_iota(jnp.int32, (256, 256), 0)
    c = lax.broadcasted_iota(jnp.int32, (256, 256), 1)
    return jnp.where((r < rank) & (c < rank), gram, jnp.where(r == c, 1.0, 0.0))


def row_masked(a, rank):
    return jnp.where(lax.broadcasted_iota(jnp.int32, a.shape, 0) < rank, a, 0.0)


def col_masked(a, rank):
    return jnp.where(lax.broadcasted_iota(jnp.int32, a.shape, 1) < rank, a, 0.0)


def tree_kernel(ranks, samples, grams, f_hbm, leaf, top, coupling, fbuf, zb, cb, tb, pairs, fsem):
    z = lax.axis_index("row")
    me = lax.axis_index("col")
    quad = lax.div(z, 4) * 4
    zq = lax.rem(z, 4)
    fcopy = pltpu.make_async_copy(f_hbm, fbuf, fsem)
    fcopy.start()

    def gram(m):
        return grams[lax.rem(m + 4 - zq, 4)]

    for m in range(4):
        zb[m] = masked(gram(m), ranks[0, quad + m])
    chol_inverse(zb, 4)
    r0 = ranks[0, z]
    w_own = split(zb[zq])
    share = dot3(split(col_masked(samples[pl.ds(pl.multiple_of(me * 32, 32), 32), :], r0)), w_own, NT)
    leaf[...] = share
    for m in range(4):
        rank = ranks[0, quad + m]
        w = split(zb[m])
        g = gram(m)
        cb[m] = dot3(w, split(row_masked(g, rank)))
        tb[m] = dot3(split(col_masked(g, rank)), w, NT)
    chain = dot3(split(share), split(cb[zq]))
    basis_t = dot3(w_own, split(col_masked(samples[...], r0)), NT)
    for n in range(2):
        pairs[n] = dot3(split(tb[2 * n]), split(cb[2 * n])) + dot3(split(tb[2 * n + 1]), split(cb[2 * n + 1]))
        zb[n] = masked(pairs[n], ranks[1, quad + 2 * n])
    chol_inverse(zb, 2)
    own = lax.div(zq, 2)
    chain = dot3(split(col_masked(chain, ranks[1, z])), split(zb[own]), NT)
    for n in range(2):
        rank = ranks[1, quad + 2 * n]
        w = split(zb[n])
        g = pairs[n]
        cb[n] = dot3(w, split(row_masked(g, rank)))
        tb[n] = dot3(split(col_masked(g, rank)), w, NT)
    chain = dot3(split(chain), split(cb[own]))
    zb[0] = masked(dot3(split(tb[0]), split(cb[0])) + dot3(split(tb[1]), split(cb[1])), ranks[2, quad])
    chol_inverse(zb, 1)
    top[...] = dot3(split(col_masked(chain, ranks[2, z])), split(zb[0]), NT)
    fcopy.wait()
    bt = split(basis_t)

    @pl.loop(0, 8)
    def _(i):
        cols = pl.ds(pl.multiple_of(i * 256, 256), 256)
        coupling[:, cols] = dot3(bt, split(fbuf[:, cols]))


def tree(ranks, samples, grams, frontal):
    vmem = pl.BlockSpec(memory_space=pltpu.VMEM)
    return pl.pallas_call(
        tree_kernel,
        out_shape=(jax.ShapeDtypeStruct((32, 256), F32), jax.ShapeDtypeStruct((32, 256), F32),
                   jax.ShapeDtypeStruct((256, 2048), F32)),
        in_specs=[pl.BlockSpec(memory_space=pltpu.SMEM), vmem, vmem, pl.BlockSpec(memory_space=pl.ANY)],
        out_specs=(vmem, vmem, vmem),
        scratch_shapes=[
            pltpu.VMEM((1024, 2048), F32),
            pltpu.VMEM((4, 256, 256), F32),
            pltpu.VMEM((4, 256, 256), F32),
            pltpu.VMEM((4, 256, 256), F32),
            pltpu.VMEM((2, 256, 256), F32),
            pltpu.SemaphoreType.DMA,
        ],
        compiler_params=pltpu.CompilerParams(vmem_limit_bytes=48 * 2**20),
        cost_estimate=pl.CostEstimate(flops=4 * 2**30, bytes_accessed=12 * 2**20, transcendentals=0),
    )(ranks, samples, grams, frontal)


def body(frontal, sketch, rank_table):
    samples, grams = gathered(frontal, sketch)
    return tree(rank_table, samples.reshape(1024, 256), grams.reshape(4, 256, 256), frontal)


def solution(mesh):
    return jax.shard_map(
        body,
        mesh=mesh,
        in_specs=(P("row", "col"), P("col", None), P()),
        out_specs=(P(("row", "col"), None), P(("row", "col"), None), P("row", "col")),
        check_vma=False,
    )
```

```python
import functools

import jax
import jax.numpy as jnp
from jax import lax
from jax.experimental import pallas as pl
from jax.experimental.pallas import tpu as pltpu
from jax.sharding import PartitionSpec as P

MESH = pl.DeviceIdType.MESH
NN = (((1,), (0,)), ((), ()))
NT = (((1,), (1,)), ((), ()))
TN = (((0,), (0,)), ((), ()))
F32 = jnp.float32


def split(x):
    hi = x.astype(jnp.bfloat16)
    return hi, (x - hi.astype(F32)).astype(jnp.bfloat16)


def dot3(a, b, dims=NN):
    ah, al = a if isinstance(a, tuple) else split(a)
    bh, bl = b if isinstance(b, tuple) else split(b)
    d = functools.partial(lax.dot_general, dimension_numbers=dims, preferred_element_type=F32)
    return d(ah, bh) + (d(ah, bl) + d(al, bh))


PB = 32
HALF = 16


def diag_inverse(x):
    lane = lax.broadcasted_iota(jnp.int32, (8, 128), 1)
    sub = lax.broadcasted_iota(jnp.int32, (8, 128), 0)
    base = (lane // PB) * PB
    m = list(x)
    n = [jnp.where(lane % PB == sub + 8 * g, 1.0, 0.0).astype(F32) for g in range(4)]
    scale = [jnp.zeros((8, 128), F32) for _ in range(4)]
    coef = [jnp.zeros((8, 128), F32) for _ in range(4)]
    for q in range(2):
        c = {}
        for k in range(HALF):
            for g in range(2 * q, 4):
                c[k, g] = jnp.take_along_axis(m[g], base + (HALF * q + k), axis=1)
        for j in range(0, HALF, 2):
            gj = 2 * q + j // 8
            s0 = j % 8

            def row(v, i):
                return jnp.broadcast_to(v[i:i + 1, :], (8, 128))

            a = row(c[j, gj], s0)
            b = row(c[j, gj], s0 + 1)
            d = row(c[j + 1, gj], s0 + 1)
            det = a * d - b * b
            rdet = 1.0 / det
            ra = 1.0 / a
            scale[gj] = jnp.where(sub == s0, lax.rsqrt(a), jnp.where(sub == s0 + 1, lax.rsqrt(det * ra), scale[gj]))
            coef[gj] = jnp.where(sub == s0 + 1, b * ra, coef[gj])
            first = {k: row(c[k, gj], s0) for k in range(j + 2, HALF)}
            second = {k: row(c[k, gj], s0 + 1) for k in range(j + 2, HALF)}
            n0, n1 = row(n[gj], s0), row(n[gj], s0 + 1)
            m0, m1 = row(m[gj], s0), row(m[gj], s0 + 1)
            for g in range(gj, 4):
                if g == gj and s0 == 6:
                    continue
                e = d * c[j, g] - b * c[j + 1, g]
                f = a * c[j + 1, g] - b * c[j, g]
                if g == gj:
                    e = jnp.where(sub > s0 + 1, e, 0.0)
                    f = jnp.where(sub > s0 + 1, f, 0.0)
                e = e * rdet
                f = f * rdet
                for k in range(j + 2, HALF):
                    c[k, g] = c[k, g] - (e * first[k] + f * second[k])
                if q == 0:
                    m[g] = m[g] - (e * m0 + f * m1)
                n[g] = n[g] - (e * n0 + f * n1)
    return [(n[g] - coef[g] * pltpu.roll(n[g], 1, 0)) * scale[g] for g in range(4)]


def place(z_ref, b, a):
    for t in range(2):
        cols = a[:, 128 * t:128 * t + 128]
        if b:
            cols = pltpu.roll(cols, 32 * b, 1)
        for s in range(8):
            dst = 128 * (s // 4) + 32 * ((s + b) % 4)
            z_ref[b, dst:dst + 32, 128 * t:128 * t + 128] = cols[32 * s:32 * s + 32]


def taken(z_ref, b):
    tiles = []
    for t in range(2):
        cols = jnp.concatenate([
            z_ref[b, 128 * (s // 4) + 32 * ((s + b) % 4):128 * (s // 4) + 32 * ((s + b) % 4) + 32, 128 * t:128 * t + 128]
            for s in range(8)], axis=0)
        if b:
            cols = pltpu.roll(cols, 128 - 32 * b, 1)
        tiles.append(cols)
    w = jnp.concatenate(tiles, axis=1)
    r = lax.broadcasted_iota(jnp.int32, (256, 256), 0)
    c = lax.broadcasted_iota(jnp.int32, (256, 256), 1)
    return jnp.where(c <= r, w, 0.0)


def chol_inverse(z_ref, batch, work=None):
    lane8 = lax.broadcasted_iota(jnp.int32, (8, 128), 1)
    lane = lax.broadcasted_iota(jnp.int32, (PB, 128), 1)
    lane96 = lax.broadcasted_iota(jnp.int32, (1, 96), 1)
    zeros = jnp.zeros((PB, 256), jnp.bfloat16)
    d = functools.partial(lax.dot_general, preferred_element_type=F32)
    for p in range(8):
        t, s = p // 4, p % 4
        tile = slice(128 * t, 128 * t + 128)
        packed = []
        for g in range(4):
            v = None
            for b in range(batch):
                at = 128 * t + 32 * ((s + b) % 4) + 8 * g
                blk = z_ref[b, at:at + 8, tile]
                v = blk if v is None else jnp.where(lane8 // PB == (s + b) % 4, blk, v)
            packed.append(v)
        w4 = jnp.concatenate(diag_inverse(packed), axis=0)
        for b in range(batch):
            turn = (s + b) % 4
            start = 128 * t + 32 * turn
            here = lane // PB == turn
            w = jnp.where(here, w4, 0.0)
            wh, wl = split(w)
            rh, rl = split(z_ref[b, start:start + PB, :])

            def padded(v):
                return jnp.concatenate([zeros] * turn + [v] + [zeros] * (3 - turn), axis=0)

            ph = padded(rh)
            u = d(wh, ph, NN) + (d(wl, ph, NN) + d(wh, padded(rl), NN))
            ut = [u[:, :128], u[:, 128:]]
            ut[t] = jnp.where(here, w4, ut[t])
            u = jnp.concatenate(ut, axis=1)
            z_ref[b, start:start + PB, :] = u
            left = [128 * (i // 4) + 32 * ((i % 4 + b) % 4) for i in range(p + 1, 8)]
            if not left:
                continue
            zt = jnp.concatenate([z_ref[b, r:r + PB, tile] for r in left], axis=0)
            zh, zl = split(zt)
            wh3 = jnp.concatenate([wh] * 3, axis=0)
            wl3 = jnp.concatenate([wl] * 3, axis=0)
            lm = d(jnp.concatenate([zh, zl], axis=1), jnp.concatenate([wh3, wh3], axis=1), NT) + d(zh, wl3, NT)
            lh, ll = split(lm)
            l96 = jnp.where(lane96 < 64, lh, ll)
            uh, ul = split(u)
            delta = d(l96, jnp.concatenate([uh, ul, uh], axis=0), NN)
            for i, r in enumerate(left):
                rows = slice(PB * i, PB * i + PB)
                for tt in range(2):
                    cols = slice(128 * tt, 128 * tt + 128)
                    old = z_ref[b, r:r + PB, cols]
                    if tt == t:
                        old = jnp.where(here, 0.0, old)
                    z_ref[b, r:r + PB, cols] = old - delta[rows, cols]


def masked(gram, rank):
    r = lax.broadcasted_iota(jnp.int32, (256, 256), 0)
    c = lax.broadcasted_iota(jnp.int32, (256, 256), 1)
    return jnp.where((r < rank) & (c < rank), gram, jnp.where(r == c, 1.0, 0.0))


def row_masked(a, rank):
    return jnp.where(lax.broadcasted_iota(jnp.int32, a.shape, 0) < rank, a, 0.0)


def col_masked(a, rank):
    return jnp.where(lax.broadcasted_iota(jnp.int32, a.shape, 1) < rank, a, 0.0)


def far_first(i):
    return lax.rem(2 + 3 * i + 3 * lax.div(i * (i - 1), 2), 4)


AROUND = ((2, 2), (2, 1), (2, 3), (1, 2), (3, 2), (1, 1), (3, 3), (1, 3), (3, 1), (2, 0), (0, 2), (1, 0), (3, 0), (0, 1), (0, 3))
BY_SOURCE = ((2, 2), (2, 1), (2, 3), (2, 0), (1, 2), (3, 2), (1, 1), (3, 3), (1, 3), (3, 1), (1, 0), (3, 0), (0, 2), (0, 1), (0, 3))


def kernel(ranks, f_hbm, s_hbm, leaf, top, coupling,
           fbuf, sbuf, sh, sl, part, xbuf, outbuf, rbuf, acc, samples, zb, pair, cb, chain, bth, btl, cbuf, hown, hother,
           fsem, ssem, xs_sem, xr_sem, rs_sem, rr_sem, as_sem, ar_sem, ws_sem, wr_sem,
           zs_sem, zr_sem, vs_sem, vr_sem, csem):
    z = lax.axis_index("row")
    me = lax.axis_index("col")
    core = lax.rem(me, 2)
    chip = lax.div(me, 2)
    x = lax.div(chip, 4)
    y = lax.rem(chip, 4)
    sibling = {"row": z, "col": chip * 2 + 1 - core}

    def chip_at(dx, dy):
        return lax.rem(x + dx, 4) * 4 + lax.rem(y + dy, 4)

    def peer(q):
        return {"row": z, "col": q * 2 + core}

    def along_z(step):
        return {"row": z + step * (1 - 2 * lax.rem(lax.div(z, step), 2)), "col": me}

    def chunk_copy(s):
        xs = lax.rem(x + far_first(s), 4)
        return pltpu.make_async_copy(f_hbm.at[pl.ds(pl.multiple_of(xs * 256, 256), 256)], fbuf.at[xs], fsem.at[s])

    def remote(src, dst, send, recv, device):
        return pltpu.make_async_remote_copy(src_ref=src, dst_ref=dst, send_sem=send, recv_sem=recv,
                                            device_id=device, device_id_type=MESH)

    scopy = pltpu.make_async_copy(s_hbm, sbuf, ssem)
    scopy.start()
    for s in range(4):
        chunk_copy(s).start()

    barrier = pltpu.get_barrier_semaphore()
    pl.semaphore_signal(barrier, inc=1, device_id=sibling, device_id_type=MESH)
    for dx, dy in AROUND:
        pl.semaphore_signal(barrier, inc=1, device_id=peer(chip_at(dx, dy)), device_id_type=MESH)
    for step in (1, 2):
        pl.semaphore_signal(barrier, inc=1, device_id=along_z(step), device_id_type=MESH)

    scopy.wait()
    sh[...], sl[...] = split(sbuf[...])
    pl.semaphore_wait(barrier, 18)

    def cores_copy(s):
        return remote(part.at[s, :, 1 - core], xbuf.at[s], xs_sem.at[s], xr_sem.at[s], sibling)

    def shard_copy(s, yy, q):
        return remote(outbuf.at[s, yy], rbuf.at[chip], rs_sem.at[q], rr_sem.at[chip], peer(q))

    @pl.loop(0, 5)
    def _(s):
        @pl.when(s < 4)
        def _():
            chunk_copy(s).wait()
            p = dot3(split(fbuf[lax.rem(x + far_first(s), 4)]), (sh[...], sl[...]))
            part[s] = p.reshape(4, 2, 32, 256)
            cores_copy(s).start()

        @pl.when(s > 0)
        def _():
            t = s - 1
            xt = lax.rem(x + far_first(t), 4)
            cores_copy(t).wait_recv()
            outbuf[t] = part[t, :, core] + xbuf[t]

            @pl.loop(0, 4)
            def _(u):
                yy = lax.rem(y + far_first(u), 4)
                q = xt * 4 + yy

                @pl.when(q != chip)
                def _():
                    shard_copy(t, yy, q).start()

    acc[...] = outbuf[3, y]
    for dx, dy in BY_SOURCE:
        q = chip_at(dx, dy)
        remote(outbuf.at[0, 0], rbuf.at[q], rs_sem.at[q], rr_sem.at[q], peer(q)).wait_recv()
        acc[...] += rbuf[q]

    samples[me] = acc[...]
    chain[...] = acc[...]

    def own_copy(q):
        return remote(samples.at[me], samples.at[me], as_sem.at[q], ar_sem.at[chip], peer(q))

    def relay_copy(q):
        return remote(samples.at[q * 2 + core], samples.at[q * 2 + core], ws_sem.at[q], wr_sem.at[q], sibling)

    for dx, dy in AROUND:
        own_copy(chip_at(dx, dy)).start()
    relay_copy(chip).start()
    for dx, dy in AROUND[::-1]:
        q = chip_at(dx, dy)
        remote(samples.at[me], samples.at[q * 2 + core], as_sem.at[q], ar_sem.at[q], peer(q)).wait_recv()
        relay_copy(q).start()

    @pl.loop(0, 16)
    def _(q):
        remote(samples.at[q * 2 + core], samples.at[q * 2 + 1 - core], ws_sem.at[q], wr_sem.at[q], sibling).wait_recv()

    full = split(samples[...].reshape(1024, 256))
    pair[...] = dot3(full, full, TN)

    def coupling_copy(i):
        cols = pl.ds(pl.multiple_of(i * 256, 256), 256)
        return pltpu.make_async_copy(cbuf.at[:, cols], coupling.at[:, cols], csem.at[i])

    def coupling_tile(i):
        cols = pl.ds(pl.multiple_of(i * 256, 256), 256)
        f = fbuf[:, :, cols].reshape(1024, 256)
        cbuf[:, cols] = dot3((bth[...], btl[...]), split(f))
        coupling_copy(i).start()

    @pl.loop(0, 3)
    def _(level):
        rank = ranks[level, z]
        place(zb, 0, masked(pair[...], rank))
        chol_inverse(zb, 1)
        w = split(taken(zb, 0))
        moved = dot3(split(col_masked(chain[...], rank)), w, NT)
        chain[...] = moved

        @pl.when(level == 0)
        def _():
            leaf[...] = chain[...]

        def z_copy():
            half = pl.ds(pl.multiple_of(core * 192, 64), 192)
            return remote(hown.at[level, half], hother.at[level, half], zs_sem.at[level], zr_sem.at[level],
                          along_z(level + 1))

        def z_relay():
            half = pl.ds(pl.multiple_of(core * 192, 64), 192)
            return remote(hother.at[level, half], hother.at[level, half], vs_sem.at[level], vr_sem.at[level], sibling)

        def z_relay_in():
            half = pl.ds(pl.multiple_of((1 - core) * 192, 64), 192)
            return remote(hother.at[level, half], hother.at[level, half], vs_sem.at[level], vr_sem.at[level], sibling)

        @pl.when(level < 2)
        def _():
            g = pair[...]
            c = split(dot3(w, split(row_masked(g, rank))))
            ct = split(dot3(split(col_masked(g, rank)), w, NT))
            h = dot3(ct, c)
            hown[level, 0:128] = h[:128, :128]
            hown[level, 128:256] = h[128:, :128]
            hown[level, 256:384] = h[128:, 128:]
            z_copy().start()
            pair[...] = h
            cb[0] = c[0]
            cb[1] = c[1]

            @pl.when(level == 0)
            def _():
                bt = dot3(w, split(col_masked(samples[...].reshape(1024, 256), rank)), NT)
                bth[...], btl[...] = split(bt)

            @pl.loop(0, 3)
            def _(i):
                coupling_tile(level * 4 + i)

            z_copy().wait_recv()
            z_relay().start()
            chain[...] = dot3(split(chain[...]), (cb[0], cb[1]))
            coupling_tile(level * 4 + 3)
            z_relay_in().wait_recv()
            o = hother[level]
            across = o[128:256]
            pair[:128, :128] += o[:128]
            pair[128:, :128] += across
            pair[:128, 128:] += across.T
            pair[128:, 128:] += o[256:]
            z_copy().wait_send()
            z_relay().wait_send()

    top[...] = chain[...]

    for s in range(4):
        cores_copy(s).wait_send()
    for dx, dy in AROUND:
        q = chip_at(dx, dy)
        shard_copy(0, 0, q).wait_send()
        own_copy(q).wait_send()

    @pl.loop(0, 16)
    def _(q):
        relay_copy(q).wait_send()

    @pl.loop(0, 8)
    def _(i):
        coupling_copy(i).wait()


def body(frontal, sketch, rank_table):
    vmem = pl.BlockSpec(memory_space=pltpu.VMEM)
    hbm = pl.BlockSpec(memory_space=pltpu.HBM)
    dma = pltpu.SemaphoreType.DMA
    bf16 = jnp.bfloat16
    return pl.pallas_call(
        kernel,
        out_shape=(jax.ShapeDtypeStruct((32, 256), F32), jax.ShapeDtypeStruct((32, 256), F32),
                   jax.ShapeDtypeStruct((256, 2048), F32)),
        in_specs=[pl.BlockSpec(memory_space=pltpu.SMEM), hbm, hbm],
        out_specs=(vmem, vmem, hbm),
        scratch_shapes=[
            pltpu.VMEM((4, 256, 2048), F32),
            pltpu.VMEM((2048, 256), F32),
            pltpu.VMEM((2048, 256), bf16),
            pltpu.VMEM((2048, 256), bf16),
            pltpu.VMEM((4, 4, 2, 32, 256), F32),
            pltpu.VMEM((4, 4, 32, 256), F32),
            pltpu.VMEM((4, 4, 32, 256), F32),
            pltpu.VMEM((16, 32, 256), F32),
            pltpu.VMEM((32, 256), F32),
            pltpu.VMEM((32, 32, 256), F32),
            pltpu.VMEM((1, 256, 256), F32),
            pltpu.VMEM((256, 256), F32),
            pltpu.VMEM((2, 256, 256), bf16),
            pltpu.VMEM((32, 256), F32),
            pltpu.VMEM((256, 1024), bf16),
            pltpu.VMEM((256, 1024), bf16),
            pltpu.VMEM((256, 2048), F32),
            pltpu.VMEM((2, 384, 128), F32),
            pltpu.VMEM((2, 384, 128), F32),
            dma((4,)), dma, dma((4,)), dma((4,)),
            dma((16,)), dma((16,)), dma((16,)), dma((16,)), dma((16,)), dma((16,)),
            dma((2,)), dma((2,)), dma((2,)), dma((2,)), dma((8,)),
        ],
        compiler_params=pltpu.CompilerParams(collective_id=0, has_side_effects=True, vmem_limit_bytes=58 * 2**20),
        cost_estimate=pl.CostEstimate(flops=7 * 2**30, bytes_accessed=12 * 2**20, transcendentals=0),
    )(rank_table, frontal, sketch)


def solution(mesh):
    return jax.shard_map(
        body,
        mesh=mesh,
        in_specs=(P("row", "col"), P("col", None), P()),
        out_specs=(P(("row", "col"), None), P(("row", "col"), None), P("row", "col")),
        check_vma=False,
    )
```

```python
import functools

import jax
import jax.numpy as jnp
from jax import lax
from jax.experimental import pallas as pl
from jax.experimental.pallas import tpu as pltpu
from jax.sharding import PartitionSpec as P

MESH = pl.DeviceIdType.MESH
NN = (((1,), (0,)), ((), ()))
NT = (((1,), (1,)), ((), ()))
TN = (((0,), (0,)), ((), ()))
F32 = jnp.float32


def split(x):
    hi = x.astype(jnp.bfloat16)
    return hi, (x - hi.astype(F32)).astype(jnp.bfloat16)


def dot3(a, b, dims=NN):
    ah, al = a if isinstance(a, tuple) else split(a)
    bh, bl = b if isinstance(b, tuple) else split(b)
    d = functools.partial(lax.dot_general, dimension_numbers=dims, preferred_element_type=F32)
    return d(ah, bh) + (d(ah, bl) + d(al, bh))


PB = 32
HALF = 16


def diag_inverse(x):
    lane = lax.broadcasted_iota(jnp.int32, (8, 128), 1)
    sub = lax.broadcasted_iota(jnp.int32, (8, 128), 0)
    base = (lane // PB) * PB
    m = list(x)
    n = [jnp.where(lane % PB == sub + 8 * g, 1.0, 0.0).astype(F32) for g in range(4)]
    scale = [jnp.zeros((8, 128), F32) for _ in range(4)]
    coef = [jnp.zeros((8, 128), F32) for _ in range(4)]
    for q in range(2):
        c = {}
        for k in range(HALF):
            for g in range(2 * q, 4):
                c[k, g] = jnp.take_along_axis(m[g], base + (HALF * q + k), axis=1)
        for j in range(0, HALF, 2):
            gj = 2 * q + j // 8
            s0 = j % 8

            def row(v, i):
                return jnp.broadcast_to(v[i:i + 1, :], (8, 128))

            a = row(c[j, gj], s0)
            b = row(c[j, gj], s0 + 1)
            d = row(c[j + 1, gj], s0 + 1)
            det = a * d - b * b
            rdet = 1.0 / det
            ra = 1.0 / a
            scale[gj] = jnp.where(sub == s0, lax.rsqrt(a), jnp.where(sub == s0 + 1, lax.rsqrt(det * ra), scale[gj]))
            coef[gj] = jnp.where(sub == s0 + 1, b * ra, coef[gj])
            first = {k: row(c[k, gj], s0) for k in range(j + 2, HALF)}
            second = {k: row(c[k, gj], s0 + 1) for k in range(j + 2, HALF)}
            n0, n1 = row(n[gj], s0), row(n[gj], s0 + 1)
            m0, m1 = row(m[gj], s0), row(m[gj], s0 + 1)
            for g in range(gj, 4):
                if g == gj and s0 == 6:
                    continue
                e = d * c[j, g] - b * c[j + 1, g]
                f = a * c[j + 1, g] - b * c[j, g]
                if g == gj:
                    e = jnp.where(sub > s0 + 1, e, 0.0)
                    f = jnp.where(sub > s0 + 1, f, 0.0)
                e = e * rdet
                f = f * rdet
                for k in range(j + 2, HALF):
                    c[k, g] = c[k, g] - (e * first[k] + f * second[k])
                if q == 0:
                    m[g] = m[g] - (e * m0 + f * m1)
                n[g] = n[g] - (e * n0 + f * n1)
    return [(n[g] - coef[g] * pltpu.roll(n[g], 1, 0)) * scale[g] for g in range(4)]


def place(z_ref, b, a):
    for t in range(2):
        cols = a[:, 128 * t:128 * t + 128]
        if b:
            cols = pltpu.roll(cols, 32 * b, 1)
        for s in range(8):
            dst = 128 * (s // 4) + 32 * ((s + b) % 4)
            z_ref[b, dst:dst + 32, 128 * t:128 * t + 128] = cols[32 * s:32 * s + 32]


def taken(z_ref, b):
    tiles = []
    for t in range(2):
        cols = jnp.concatenate([
            z_ref[b, 128 * (s // 4) + 32 * ((s + b) % 4):128 * (s // 4) + 32 * ((s + b) % 4) + 32, 128 * t:128 * t + 128]
            for s in range(8)], axis=0)
        if b:
            cols = pltpu.roll(cols, 128 - 32 * b, 1)
        tiles.append(cols)
    w = jnp.concatenate(tiles, axis=1)
    r = lax.broadcasted_iota(jnp.int32, (256, 256), 0)
    c = lax.broadcasted_iota(jnp.int32, (256, 256), 1)
    return jnp.where(c <= r, w, 0.0)


def chol_inverse(z_ref, batch, work=None):
    lane8 = lax.broadcasted_iota(jnp.int32, (8, 128), 1)
    lane = lax.broadcasted_iota(jnp.int32, (PB, 128), 1)
    lane96 = lax.broadcasted_iota(jnp.int32, (1, 96), 1)
    zeros = jnp.zeros((PB, 256), jnp.bfloat16)
    d = functools.partial(lax.dot_general, preferred_element_type=F32)
    for p in range(8):
        t, s = p // 4, p % 4
        tile = slice(128 * t, 128 * t + 128)
        packed = []
        for g in range(4):
            v = None
            for b in range(batch):
                at = 128 * t + 32 * ((s + b) % 4) + 8 * g
                blk = z_ref[b, at:at + 8, tile]
                v = blk if v is None else jnp.where(lane8 // PB == (s + b) % 4, blk, v)
            packed.append(v)
        w4 = jnp.concatenate(diag_inverse(packed), axis=0)
        for b in range(batch):
            turn = (s + b) % 4
            start = 128 * t + 32 * turn
            here = lane // PB == turn
            w = jnp.where(here, w4, 0.0)
            wh, wl = split(w)
            rh, rl = split(z_ref[b, start:start + PB, :])

            def padded(v):
                return jnp.concatenate([zeros] * turn + [v] + [zeros] * (3 - turn), axis=0)

            ph = padded(rh)
            u = d(wh, ph, NN) + (d(wl, ph, NN) + d(wh, padded(rl), NN))
            ut = [u[:, :128], u[:, 128:]]
            ut[t] = jnp.where(here, w4, ut[t])
            u = jnp.concatenate(ut, axis=1)
            z_ref[b, start:start + PB, :] = u
            left = [128 * (i // 4) + 32 * ((i % 4 + b) % 4) for i in range(p + 1, 8)]
            if not left:
                continue
            zt = jnp.concatenate([z_ref[b, r:r + PB, tile] for r in left], axis=0)
            zh, zl = split(zt)
            wh3 = jnp.concatenate([wh] * 3, axis=0)
            wl3 = jnp.concatenate([wl] * 3, axis=0)
            lm = d(jnp.concatenate([zh, zl], axis=1), jnp.concatenate([wh3, wh3], axis=1), NT) + d(zh, wl3, NT)
            lh, ll = split(lm)
            l96 = jnp.where(lane96 < 64, lh, ll)
            uh, ul = split(u)
            delta = d(l96, jnp.concatenate([uh, ul, uh], axis=0), NN)
            for i, r in enumerate(left):
                rows = slice(PB * i, PB * i + PB)
                for tt in range(2):
                    cols = slice(128 * tt, 128 * tt + 128)
                    old = z_ref[b, r:r + PB, cols]
                    if tt == t:
                        old = jnp.where(here, 0.0, old)
                    z_ref[b, r:r + PB, cols] = old - delta[rows, cols]


def masked(gram, rank):
    r = lax.broadcasted_iota(jnp.int32, (256, 256), 0)
    c = lax.broadcasted_iota(jnp.int32, (256, 256), 1)
    return jnp.where((r < rank) & (c < rank), gram, jnp.where(r == c, 1.0, 0.0))


def row_masked(a, rank):
    return jnp.where(lax.broadcasted_iota(jnp.int32, a.shape, 0) < rank, a, 0.0)


def col_masked(a, rank):
    return jnp.where(lax.broadcasted_iota(jnp.int32, a.shape, 1) < rank, a, 0.0)


def far_first(i):
    return lax.rem(2 + 3 * i + 3 * lax.div(i * (i - 1), 2), 4)


AROUND = ((2, 2), (2, 1), (2, 3), (1, 2), (3, 2), (1, 1), (3, 3), (1, 3), (3, 1), (2, 0), (0, 2), (1, 0), (3, 0), (0, 1), (0, 3))
BY_SOURCE = ((2, 2), (2, 1), (2, 3), (2, 0), (1, 2), (3, 2), (1, 1), (3, 3), (1, 3), (3, 1), (1, 0), (3, 0), (0, 2), (0, 1), (0, 3))


def kernel(ranks, f_hbm, s_hbm, leaf, coupling, pair, chain,
           fbuf, sbuf, sh, sl, part, xbuf, outbuf, rbuf, acc, samples, zb, cb, bth, btl, hown, hother,
           fsem, ssem, xs_sem, xr_sem, rs_sem, rr_sem, as_sem, ar_sem, ws_sem, wr_sem,
           zs_sem, zr_sem, vs_sem, vr_sem):
    z = lax.axis_index("row")
    me = lax.axis_index("col")
    core = lax.rem(me, 2)
    chip = lax.div(me, 2)
    x = lax.div(chip, 4)
    y = lax.rem(chip, 4)
    sibling = {"row": z, "col": chip * 2 + 1 - core}

    def chip_at(dx, dy):
        return lax.rem(x + dx, 4) * 4 + lax.rem(y + dy, 4)

    def peer(q):
        return {"row": z, "col": q * 2 + core}

    def along_z(step):
        return {"row": z + step * (1 - 2 * lax.rem(lax.div(z, step), 2)), "col": me}

    def chunk_copy(s):
        xs = lax.rem(x + far_first(s), 4)
        return pltpu.make_async_copy(f_hbm.at[pl.ds(pl.multiple_of(xs * 256, 256), 256)], fbuf.at[xs], fsem.at[s])

    def remote(src, dst, send, recv, device):
        return pltpu.make_async_remote_copy(src_ref=src, dst_ref=dst, send_sem=send, recv_sem=recv,
                                            device_id=device, device_id_type=MESH)

    scopy = pltpu.make_async_copy(s_hbm, sbuf, ssem)
    scopy.start()
    for s in range(4):
        chunk_copy(s).start()

    barrier = pltpu.get_barrier_semaphore()
    pl.semaphore_signal(barrier, inc=1, device_id=sibling, device_id_type=MESH)
    for dx, dy in AROUND:
        pl.semaphore_signal(barrier, inc=1, device_id=peer(chip_at(dx, dy)), device_id_type=MESH)
    for step in (1, 2):
        pl.semaphore_signal(barrier, inc=1, device_id=along_z(step), device_id_type=MESH)

    scopy.wait()
    sh[...], sl[...] = split(sbuf[...])

    def cores_copy(s):
        return remote(part.at[s, :, 1 - core], xbuf.at[s], xs_sem.at[s], xr_sem.at[s], sibling)

    def shard_copy(s, yy, q):
        return remote(outbuf.at[s, yy], rbuf.at[chip], rs_sem.at[q], rr_sem.at[chip], peer(q))

    @pl.loop(0, 5)
    def _(s):
        @pl.when(s < 4)
        def _():
            chunk_copy(s).wait()
            p = dot3(split(fbuf[lax.rem(x + far_first(s), 4)]), (sh[...], sl[...]))
            part[s] = p.reshape(4, 2, 32, 256)

            @pl.when(s == 0)
            def _():
                pl.semaphore_wait(barrier, 18)

            cores_copy(s).start()

        @pl.when(s > 0)
        def _():
            t = s - 1
            xt = lax.rem(x + far_first(t), 4)
            cores_copy(t).wait_recv()
            outbuf[t] = part[t, :, core] + xbuf[t]

            @pl.loop(0, 4)
            def _(u):
                yy = lax.rem(y + far_first(u), 4)
                q = xt * 4 + yy

                @pl.when(q != chip)
                def _():
                    shard_copy(t, yy, q).start()

    acc[...] = outbuf[3, y]
    for dx, dy in BY_SOURCE:
        q = chip_at(dx, dy)
        remote(outbuf.at[0, 0], rbuf.at[q], rs_sem.at[q], rr_sem.at[q], peer(q)).wait_recv()
        acc[...] += rbuf[q]

    samples[me] = acc[...]
    chain[...] = acc[...]

    def own_copy(q):
        return remote(samples.at[me], samples.at[me], as_sem.at[q], ar_sem.at[chip], peer(q))

    def relay_copy(q):
        return remote(samples.at[q * 2 + core], samples.at[q * 2 + core], ws_sem.at[q], wr_sem.at[q], sibling)

    for dx, dy in AROUND:
        own_copy(chip_at(dx, dy)).start()
    relay_copy(chip).start()
    for dx, dy in AROUND[::-1]:
        q = chip_at(dx, dy)
        remote(samples.at[me], samples.at[q * 2 + core], as_sem.at[q], ar_sem.at[q], peer(q)).wait_recv()
        relay_copy(q).start()

    @pl.loop(0, 16)
    def _(q):
        remote(samples.at[q * 2 + core], samples.at[q * 2 + 1 - core], ws_sem.at[q], wr_sem.at[q], sibling).wait_recv()

    full = split(samples[...].reshape(1024, 256))
    pair[...] = dot3(full, full, TN)

    def coupling_tile(i):
        cols = pl.ds(pl.multiple_of(i * 256, 256), 256)
        f = fbuf[:, :, cols].reshape(1024, 256)
        coupling[:, cols] = dot3((bth[...], btl[...]), split(f))

    @pl.loop(0, 2)
    def _(level):
        rank = ranks[level, z]
        place(zb, 0, masked(pair[...], rank))
        chol_inverse(zb, 1)
        w = split(taken(zb, 0))
        moved = dot3(split(col_masked(chain[...], rank)), w, NT)
        chain[...] = moved

        @pl.when(level == 0)
        def _():
            leaf[...] = chain[...]

        def z_copy():
            half = pl.ds(pl.multiple_of(core * 192, 64), 192)
            return remote(hown.at[level, half], hother.at[level, half], zs_sem.at[level], zr_sem.at[level],
                          along_z(level + 1))

        def z_relay():
            half = pl.ds(pl.multiple_of(core * 192, 64), 192)
            return remote(hother.at[level, half], hother.at[level, half], vs_sem.at[level], vr_sem.at[level], sibling)

        def z_relay_in():
            half = pl.ds(pl.multiple_of((1 - core) * 192, 64), 192)
            return remote(hother.at[level, half], hother.at[level, half], vs_sem.at[level], vr_sem.at[level], sibling)

        g = pair[...]
        c = split(dot3(w, split(row_masked(g, rank))))
        ct = split(dot3(split(col_masked(g, rank)), w, NT))
        h = dot3(ct, c)
        hown[level, 0:128] = h[:128, :128]
        hown[level, 128:256] = h[128:, :128]
        hown[level, 256:384] = h[128:, 128:]
        z_copy().start()
        pair[...] = h
        cb[0] = c[0]
        cb[1] = c[1]

        @pl.when(level == 0)
        def _():
            bt = dot3(w, split(col_masked(samples[...].reshape(1024, 256), rank)), NT)
            bth[...], btl[...] = split(bt)

        @pl.loop(0, 3)
        def _(i):
            coupling_tile(level * 4 + i)

        z_copy().wait_recv()
        z_relay().start()
        chain[...] = dot3(split(chain[...]), (cb[0], cb[1]))
        coupling_tile(level * 4 + 3)
        z_relay_in().wait_recv()
        o = hother[level]
        across = o[128:256]
        pair[:128, :128] += o[:128]
        pair[128:, :128] += across
        pair[:128, 128:] += across.T
        pair[128:, 128:] += o[256:]
        z_copy().wait_send()
        z_relay().wait_send()

    for s in range(4):
        cores_copy(s).wait_send()
    for dx, dy in AROUND:
        q = chip_at(dx, dy)
        shard_copy(0, 0, q).wait_send()
        own_copy(q).wait_send()

    @pl.loop(0, 16)
    def _(q):
        relay_copy(q).wait_send()


def last_kernel(ranks, leaf_in, coupling_in, pair, chain, leaf, top, coupling, zb, sem):
    copies = [pltpu.make_async_copy(coupling_in, coupling, sem.at[0]), pltpu.make_async_copy(leaf_in, leaf, sem.at[1])]
    for copy in copies:
        copy.start()
    rank = ranks[2, lax.axis_index("row")]
    place(zb, 0, masked(pair[...], rank))
    chol_inverse(zb, 1)
    top[...] = dot3(split(col_masked(chain[...], rank)), split(taken(zb, 0)), NT)
    for copy in copies:
        copy.wait()


def body(frontal, sketch, rank_table):
    vmem = pl.BlockSpec(memory_space=pltpu.VMEM)
    hbm = pl.BlockSpec(memory_space=pltpu.HBM)
    dma = pltpu.SemaphoreType.DMA
    bf16 = jnp.bfloat16
    smem = pl.BlockSpec(memory_space=pltpu.SMEM)
    frontal = pltpu.with_memory_space_constraint(frontal, pltpu.HBM)
    sketch = pltpu.with_memory_space_constraint(sketch, pltpu.HBM)
    held = pl.pallas_call(
        kernel,
        out_shape=(pltpu.VMEM((32, 256), F32), pltpu.VMEM((256, 2048), F32), pltpu.VMEM((256, 256), F32), pltpu.VMEM((32, 256), F32)),
        in_specs=[smem, hbm, hbm],
        out_specs=(vmem, vmem, vmem, vmem),
        scratch_shapes=[
            pltpu.VMEM((4, 256, 2048), F32),
            pltpu.VMEM((2048, 256), F32),
            pltpu.VMEM((2048, 256), bf16),
            pltpu.VMEM((2048, 256), bf16),
            pltpu.VMEM((4, 4, 2, 32, 256), F32),
            pltpu.VMEM((4, 4, 32, 256), F32),
            pltpu.VMEM((4, 4, 32, 256), F32),
            pltpu.VMEM((16, 32, 256), F32),
            pltpu.VMEM((32, 256), F32),
            pltpu.VMEM((32, 32, 256), F32),
            pltpu.VMEM((1, 256, 256), F32),
            pltpu.VMEM((2, 256, 256), bf16),
            pltpu.VMEM((256, 1024), bf16),
            pltpu.VMEM((256, 1024), bf16),
            pltpu.VMEM((2, 384, 128), F32),
            pltpu.VMEM((2, 384, 128), F32),
            dma((4,)), dma, dma((4,)), dma((4,)),
            dma((16,)), dma((16,)), dma((16,)), dma((16,)), dma((16,)), dma((16,)),
            dma((2,)), dma((2,)), dma((2,)), dma((2,)),
        ],
        compiler_params=pltpu.CompilerParams(collective_id=0, has_side_effects=True, vmem_limit_bytes=40 * 2**20),
        cost_estimate=pl.CostEstimate(flops=7 * 2**30, bytes_accessed=12 * 2**20, transcendentals=0),
    )(rank_table, frontal, sketch)
    return pl.pallas_call(
        last_kernel,
        out_shape=(jax.ShapeDtypeStruct((32, 256), F32), jax.ShapeDtypeStruct((32, 256), F32),
                   jax.ShapeDtypeStruct((256, 2048), F32)),
        in_specs=[smem, vmem, vmem, vmem, vmem],
        out_specs=(hbm, vmem, hbm),
        scratch_shapes=[pltpu.VMEM((1, 256, 256), F32), dma((2,))],
        compiler_params=pltpu.CompilerParams(vmem_limit_bytes=16 * 2**20),
    )(rank_table, *held)


def solution(mesh):
    return jax.shard_map(
        body,
        mesh=mesh,
        in_specs=(P("row", "col"), P("col", None), P()),
        out_specs=(P(("row", "col"), None), P(("row", "col"), None), P("row", "col")),
        check_vma=False,
    )
```

```python
import functools

import jax
import jax.numpy as jnp
from jax import lax
from jax.experimental import pallas as pl
from jax.experimental.pallas import tpu as pltpu
from jax.sharding import PartitionSpec as P

MESH = pl.DeviceIdType.MESH
NN = (((1,), (0,)), ((), ()))
NT = (((1,), (1,)), ((), ()))
TN = (((0,), (0,)), ((), ()))
F32 = jnp.float32


def split(x):
    hi = x.astype(jnp.bfloat16)
    return hi, (x - hi.astype(F32)).astype(jnp.bfloat16)


def dot3(a, b, dims=NN):
    ah, al = a if isinstance(a, tuple) else split(a)
    bh, bl = b if isinstance(b, tuple) else split(b)
    d = functools.partial(lax.dot_general, dimension_numbers=dims, preferred_element_type=F32)
    return d(ah, bh) + (d(ah, bl) + d(al, bh))


PB = 32
HALF = 16


def panel_inverse(x, s):
    lane = lax.broadcasted_iota(jnp.int32, (8, 128), 1)
    sub = lax.broadcasted_iota(jnp.int32, (8, 128), 0)
    m = list(x)
    n = [jnp.where(lane == sub + (8 * g + PB * s), 1.0, 0.0).astype(F32) for g in range(4)]
    scale = [jnp.zeros((8, 128), F32) for _ in range(4)]
    coef = [jnp.zeros((8, 128), F32) for _ in range(4)]
    for q in range(2):
        c = {}
        for k in range(HALF):
            for g in range(2 * q, 4):
                at = PB * s + HALF * q + k
                c[k, g] = jnp.take_along_axis(m[g], lane * 0 + at, axis=1)
        for j in range(0, HALF, 2):
            gj = 2 * q + j // 8
            s0 = j % 8

            def row(v, i):
                return jnp.broadcast_to(v[i:i + 1, :], (8, 128))

            a = row(c[j, gj], s0)
            b = row(c[j, gj], s0 + 1)
            d = row(c[j + 1, gj], s0 + 1)
            det = a * d - b * b
            rdet = 1.0 / det
            ra = 1.0 / a
            scale[gj] = jnp.where(sub == s0, lax.rsqrt(a), jnp.where(sub == s0 + 1, lax.rsqrt(det * ra), scale[gj]))
            coef[gj] = jnp.where(sub == s0 + 1, b * ra, coef[gj])
            first = {k: row(c[k, gj], s0) for k in range(j + 2, HALF)}
            second = {k: row(c[k, gj], s0 + 1) for k in range(j + 2, HALF)}
            n0, n1 = row(n[gj], s0), row(n[gj], s0 + 1)
            m0, m1 = row(m[gj], s0), row(m[gj], s0 + 1)
            for g in range(gj, 4):
                if g == gj and s0 == 6:
                    continue
                e = d * c[j, g] - b * c[j + 1, g]
                f = a * c[j + 1, g] - b * c[j, g]
                if g == gj:
                    e = jnp.where(sub > s0 + 1, e, 0.0)
                    f = jnp.where(sub > s0 + 1, f, 0.0)
                e = e * rdet
                f = f * rdet
                for k in range(j + 2, HALF):
                    c[k, g] = c[k, g] - (e * first[k] + f * second[k])
                if q == 0:
                    m[g] = m[g] - (e * m0 + f * m1)
                n[g] = n[g] - (e * n0 + f * n1)
    return [(n[g] - coef[g] * pltpu.roll(n[g], 1, 0)) * scale[g] for g in range(4)]


def chol_inverse(z_ref, between):
    here_lane = lax.broadcasted_iota(jnp.int32, (PB, 128), 1)
    lane96 = lax.broadcasted_iota(jnp.int32, (1, 96), 1)
    zeros = jnp.zeros((PB, 128), jnp.bfloat16)
    d = functools.partial(lax.dot_general, preferred_element_type=F32)
    for s in range(4):
        start = PB * s
        w = jnp.concatenate(panel_inverse([z_ref[start + 8 * g:start + 8 * g + 8, :] for g in range(4)], s), axis=0)
        here = here_lane // PB == s
        wh, wl = split(w)
        rh, rl = split(z_ref[start:start + PB, :])

        def padded(v):
            return jnp.concatenate([zeros] * s + [v] + [zeros] * (3 - s), axis=0)

        u = d(wh, padded(rh), NN) + (d(wl, padded(rh), NN) + d(wh, padded(rl), NN))
        u = jnp.where(here, w, u)
        if s < 3:
            below = slice(start + PB, 128)
            z = z_ref[below, :]
            zh, zl = split(z)
            wh3 = jnp.concatenate([wh] * 3, axis=0)
            wl3 = jnp.concatenate([wl] * 3, axis=0)
            lm = d(jnp.concatenate([zh, zl], axis=1), jnp.concatenate([wh3, wh3], axis=1), NT) + d(zh, wl3, NT)
            lh, ll = split(lm)
            uh, ul = split(u)
            delta = d(jnp.where(lane96 < 64, lh, ll), jnp.concatenate([uh, ul, uh], axis=0), NN)
            z_ref[below, :] = jnp.where(here_lane[:1] // PB == s, 0.0, z) - delta
        z_ref[start:start + PB, :] = u
        between(s)


def lower(a):
    r = lax.broadcasted_iota(jnp.int32, a.shape, 0)
    c = lax.broadcasted_iota(jnp.int32, a.shape, 1)
    return jnp.where(c <= r, a, 0.0)


def nothing(s):
    pass


def schur(z_ref, w11, a21, a22):
    l21 = split(dot3(split(a21), w11, NT))
    z_ref[...] = a22 - dot3(l21, l21, NT)
    return -dot3(l21, w11)


def masked(a, rank, row0, col0):
    r = lax.broadcasted_iota(jnp.int32, a.shape, 0) + row0
    c = lax.broadcasted_iota(jnp.int32, a.shape, 1) + col0
    return jnp.where((r < rank) & (c < rank), a, jnp.where(r == c, 1.0, 0.0))


def row_masked(a, rank):
    return jnp.where(lax.broadcasted_iota(jnp.int32, a.shape, 0) < rank, a, 0.0)


def col_masked(a, rank):
    return jnp.where(lax.broadcasted_iota(jnp.int32, a.shape, 1) < rank, a, 0.0)


def far_first(i):
    return lax.rem(2 + 3 * i + 3 * lax.div(i * (i - 1), 2), 4)


AROUND = ((2, 2), (2, 1), (2, 3), (1, 2), (3, 2), (1, 1), (3, 3), (1, 3), (3, 1), (2, 0), (0, 2), (1, 0), (3, 0), (0, 1), (0, 3))
BY_SOURCE = ((2, 2), (2, 1), (2, 3), (2, 0), (1, 2), (3, 2), (1, 1), (3, 3), (1, 3), (3, 1), (1, 0), (3, 0), (0, 2), (0, 1), (0, 3))


def kernel(ranks, f_hbm, s_hbm, leaf, coupling, w11_out, pair, chain,
           fbuf, sbuf, sh, sl, part, xbuf, outbuf, rbuf, acc, samples, zb, wb, gb, cb, bth, btl, hown, hother,
           fsem, ssem, xs_sem, xr_sem, rs_sem, rr_sem, as_sem, ar_sem, ws_sem, wr_sem,
           zs_sem, zr_sem, vs_sem, vr_sem):
    z = lax.axis_index("row")
    me = lax.axis_index("col")
    core = lax.rem(me, 2)
    chip = lax.div(me, 2)
    x = lax.div(chip, 4)
    y = lax.rem(chip, 4)
    sibling = {"row": z, "col": chip * 2 + 1 - core}

    def chip_at(dx, dy):
        return lax.rem(x + dx, 4) * 4 + lax.rem(y + dy, 4)

    def peer(q):
        return {"row": z, "col": q * 2 + core}

    def along_z(step):
        return {"row": z + step * (1 - 2 * lax.rem(lax.div(z, step), 2)), "col": me}

    def chunk_copy(s):
        xs = lax.rem(x + far_first(s), 4)
        return pltpu.make_async_copy(f_hbm.at[pl.ds(pl.multiple_of(xs * 256, 256), 256)], fbuf.at[xs], fsem.at[s])

    def remote(src, dst, send, recv, device):
        return pltpu.make_async_remote_copy(src_ref=src, dst_ref=dst, send_sem=send, recv_sem=recv,
                                            device_id=device, device_id_type=MESH)

    scopy = pltpu.make_async_copy(s_hbm, sbuf, ssem)
    scopy.start()
    for s in range(4):
        chunk_copy(s).start()

    barrier = pltpu.get_barrier_semaphore()
    pl.semaphore_signal(barrier, inc=1, device_id=sibling, device_id_type=MESH)
    for dx, dy in AROUND:
        pl.semaphore_signal(barrier, inc=1, device_id=peer(chip_at(dx, dy)), device_id_type=MESH)
    for step in (1, 2):
        pl.semaphore_signal(barrier, inc=1, device_id=along_z(step), device_id_type=MESH)

    scopy.wait()
    sh[...], sl[...] = split(sbuf[...])

    def cores_copy(s):
        return remote(part.at[s, :, 1 - core], xbuf.at[s], xs_sem.at[s], xr_sem.at[s], sibling)

    def shard_copy(s, yy, q):
        return remote(outbuf.at[s, yy], rbuf.at[chip], rs_sem.at[q], rr_sem.at[chip], peer(q))

    @pl.loop(0, 5)
    def _(s):
        @pl.when(s < 4)
        def _():
            chunk_copy(s).wait()
            p = dot3(split(fbuf[lax.rem(x + far_first(s), 4)]), (sh[...], sl[...]))
            part[s] = p.reshape(4, 2, 32, 256)

            @pl.when(s == 0)
            def _():
                pl.semaphore_wait(barrier, 18)

            cores_copy(s).start()

        @pl.when(s > 0)
        def _():
            t = s - 1
            xt = lax.rem(x + far_first(t), 4)
            cores_copy(t).wait_recv()
            outbuf[t] = part[t, :, core] + xbuf[t]

            @pl.loop(0, 4)
            def _(u):
                yy = lax.rem(y + far_first(u), 4)
                q = xt * 4 + yy

                @pl.when(q != chip)
                def _():
                    shard_copy(t, yy, q).start()

    acc[...] = outbuf[3, y]
    for dx, dy in BY_SOURCE:
        q = chip_at(dx, dy)
        remote(outbuf.at[0, 0], rbuf.at[q], rs_sem.at[q], rr_sem.at[q], peer(q)).wait_recv()
        acc[...] += rbuf[q]

    chain[...] = acc[...]
    for h in range(2):
        samples[h, me] = acc[:, 128 * h:128 * h + 128]

    def own_copy(h, q):
        return remote(samples.at[h, me], samples.at[h, me], as_sem.at[h, q], ar_sem.at[h, chip], peer(q))

    def relay_copy(h, q):
        return remote(samples.at[h, q * 2 + core], samples.at[h, q * 2 + core], ws_sem.at[h, q], wr_sem.at[h, q], sibling)

    for h in range(2):
        for dx, dy in AROUND:
            own_copy(h, chip_at(dx, dy)).start()
        relay_copy(h, chip).start()

    def relay_half(h):
        for dx, dy in AROUND[::-1]:
            q = chip_at(dx, dy)
            remote(samples.at[h, me], samples.at[h, q * 2 + core], as_sem.at[h, q], ar_sem.at[h, q], peer(q)).wait_recv()
            relay_copy(h, q).start()

    def half_arrived(h):
        @pl.loop(0, 16)
        def _(q):
            remote(samples.at[h, q * 2 + core], samples.at[h, q * 2 + 1 - core], ws_sem.at[h, q], wr_sem.at[h, q],
                   sibling).wait_recv()

    def half_samples(h):
        return split(samples[h].reshape(1024, 128))

    def rows_of(piece, c):
        if piece == 0:
            return pl.ds(pl.multiple_of(c * 64, 64), 64)
        return pl.ds(pl.multiple_of(128 + c * 128, 128), 128)

    def z_copy(level, piece):
        at = rows_of(piece, core)
        i = level * 2 + piece
        return remote(hown.at[level, at], hother.at[level, at], zs_sem.at[i], zr_sem.at[i], along_z(level + 1))

    def z_relay(level, piece, c):
        at = rows_of(piece, c)
        i = level * 2 + piece
        return remote(hother.at[level, at], hother.at[level, at], vs_sem.at[i], vr_sem.at[i], sibling)

    relay_half(0)
    half_arrived(0)
    first = half_samples(0)
    pair[0] = dot3(first, first, TN)

    def coupling_tile(i):
        cols = pl.ds(pl.multiple_of(i * 256, 256), 256)
        f = fbuf[:, :, cols].reshape(1024, 256)
        coupling[:, cols] = dot3((bth[...], btl[...]), split(f))

    @pl.loop(0, 3)
    def _(level):
        rank = ranks[level, z]
        zb[...] = masked(pair[0], rank, 0, 0)

        def between(s):
            if s == 1:
                @pl.when(level == 0)
                def _():
                    relay_half(1)

                @pl.when(level > 0)
                def _():
                    z_copy(level - 1, 1).wait_recv()
                    z_relay(level - 1, 1, core).start()

        chol_inverse(zb, between)
        w11_out[...] = lower(zb[...])

        @pl.when(level == 0)
        def _():
            half_arrived(1)
            left, right = half_samples(0), half_samples(1)
            pair[1] = dot3(right, left, TN)
            pair[2] = dot3(right, right, TN)

        @pl.when(level > 0)
        def _():
            z_relay(level - 1, 1, 1 - core).wait_recv()
            pair[1] += hother[level - 1, 128:256]
            pair[2] += hother[level - 1, 256:384]
            for piece in range(2):
                z_copy(level - 1, piece).wait_send()
                z_relay(level - 1, piece, core).wait_send()

        @pl.when(level < 2)
        def _():
            w11 = w11_out[...]
            m21 = schur(zb, split(w11), masked(pair[1], rank, 128, 0), masked(pair[2], rank, 128, 128))
            gb[:128, :128] = pair[0]
            gb[:128, 128:] = pair[1].T
            gb[128:, :128] = pair[1]
            gb[128:, 128:] = pair[2]
            chol_inverse(zb, nothing)
            w22 = lower(zb[...])
            wb[:128, :128] = w11
            wb[:128, 128:] = jnp.zeros((128, 128), F32)
            wb[128:, :128] = dot3(w22, m21)
            wb[128:, 128:] = w22
            w = split(wb[...])
            g = gb[...]
            c = split(dot3(w, split(row_masked(g, rank))))
            ct = split(dot3(split(col_masked(g, rank)), w, NT))

            def block(i, j):
                a, b = slice(128 * i, 128 * i + 128), slice(128 * j, 128 * j + 128)
                return dot3((ct[0][a], ct[1][a]), (c[0][:, b], c[1][:, b]))

            h11 = block(0, 0)
            hown[level, 0:128] = h11
            z_copy(level, 0).start()
            h21, h22 = block(1, 0), block(1, 1)
            hown[level, 128:256] = h21
            hown[level, 256:384] = h22
            z_copy(level, 1).start()
            pair[0] = h11
            pair[1] = h21
            pair[2] = h22
            cb[0] = c[0]
            cb[1] = c[1]
            moved = dot3(split(col_masked(chain[...], rank)), w, NT)
            chain[...] = moved

            @pl.when(level == 0)
            def _():
                leaf[...] = chain[...]
                w0 = split(wb[...])
                whole = col_masked(jnp.concatenate([samples[0].reshape(1024, 128), samples[1].reshape(1024, 128)], axis=1), rank)
                bth[...], btl[...] = split(dot3(w0, split(whole), NT))

            @pl.loop(0, 3)
            def _(i):
                coupling_tile(level * 4 + i)

            z_copy(level, 0).wait_recv()
            z_relay(level, 0, core).start()
            chain[...] = dot3(split(chain[...]), (cb[0], cb[1]))
            coupling_tile(level * 4 + 3)
            z_relay(level, 0, 1 - core).wait_recv()
            pair[0] += hother[level, 0:128]

    for s in range(4):
        cores_copy(s).wait_send()
    for dx, dy in AROUND:
        q = chip_at(dx, dy)
        shard_copy(0, 0, q).wait_send()
        own_copy(0, q).wait_send()
        own_copy(1, q).wait_send()

    @pl.loop(0, 16)
    def _(q):
        relay_copy(0, q).wait_send()
        relay_copy(1, q).wait_send()


def last_kernel(ranks, leaf_in, coupling_in, w11, pair, chain, leaf, top, coupling, zb, sem):
    copies = [pltpu.make_async_copy(coupling_in, coupling, sem.at[0]), pltpu.make_async_copy(leaf_in, leaf, sem.at[1])]
    for copy in copies:
        copy.start()
    rank = ranks[2, lax.axis_index("row")]
    w = split(w11[...])
    m21 = split(schur(zb, w, masked(pair[1], rank, 128, 0), masked(pair[2], rank, 128, 128)))
    t = col_masked(chain[...], rank)
    left = split(t[:, :128])
    right = t[:, 128:] + dot3(left, m21, NT)
    chol_inverse(zb, nothing)
    top[:, :128] = dot3(left, w, NT)
    top[:, 128:] = dot3(split(right), split(lower(zb[...])), NT)
    for copy in copies:
        copy.wait()


def body(frontal, sketch, rank_table):
    vmem = pl.BlockSpec(memory_space=pltpu.VMEM)
    hbm = pl.BlockSpec(memory_space=pltpu.HBM)
    dma = pltpu.SemaphoreType.DMA
    bf16 = jnp.bfloat16
    smem = pl.BlockSpec(memory_space=pltpu.SMEM)
    frontal = pltpu.with_memory_space_constraint(frontal, pltpu.HBM)
    sketch = pltpu.with_memory_space_constraint(sketch, pltpu.HBM)
    held = pl.pallas_call(
        kernel,
        out_shape=(pltpu.VMEM((32, 256), F32), pltpu.VMEM((256, 2048), F32), pltpu.VMEM((128, 128), F32),
                   pltpu.VMEM((3, 128, 128), F32), pltpu.VMEM((32, 256), F32)),
        in_specs=[smem, hbm, hbm],
        out_specs=(vmem,) * 5,
        scratch_shapes=[
            pltpu.VMEM((4, 256, 2048), F32),
            pltpu.VMEM((2048, 256), F32),
            pltpu.VMEM((2048, 256), bf16),
            pltpu.VMEM((2048, 256), bf16),
            pltpu.VMEM((4, 4, 2, 32, 256), F32),
            pltpu.VMEM((4, 4, 32, 256), F32),
            pltpu.VMEM((4, 4, 32, 256), F32),
            pltpu.VMEM((16, 32, 256), F32),
            pltpu.VMEM((32, 256), F32),
            pltpu.VMEM((2, 32, 32, 128), F32),
            pltpu.VMEM((128, 128), F32),
            pltpu.VMEM((256, 256), F32),
            pltpu.VMEM((256, 256), F32),
            pltpu.VMEM((2, 256, 256), bf16),
            pltpu.VMEM((256, 1024), bf16),
            pltpu.VMEM((256, 1024), bf16),
            pltpu.VMEM((2, 384, 128), F32),
            pltpu.VMEM((2, 384, 128), F32),
            dma((4,)), dma, dma((4,)), dma((4,)),
            dma((16,)), dma((16,)), dma((2, 16)), dma((2, 16)), dma((2, 16)), dma((2, 16)),
            dma((4,)), dma((4,)), dma((4,)), dma((4,)),
        ],
        compiler_params=pltpu.CompilerParams(collective_id=0, has_side_effects=True, vmem_limit_bytes=40 * 2**20),
        cost_estimate=pl.CostEstimate(flops=7 * 2**30, bytes_accessed=12 * 2**20, transcendentals=0),
    )(rank_table, frontal, sketch)
    return pl.pallas_call(
        last_kernel,
        out_shape=(jax.ShapeDtypeStruct((32, 256), F32), jax.ShapeDtypeStruct((32, 256), F32),
                   jax.ShapeDtypeStruct((256, 2048), F32)),
        in_specs=[smem] + [vmem] * 5,
        out_specs=(hbm, vmem, hbm),
        scratch_shapes=[pltpu.VMEM((128, 128), F32), dma((2,))],
        compiler_params=pltpu.CompilerParams(vmem_limit_bytes=16 * 2**20),
    )(rank_table, *held)


def solution(mesh):
    return jax.shard_map(
        body,
        mesh=mesh,
        in_specs=(P("row", "col"), P("col", None), P()),
        out_specs=(P(("row", "col"), None), P(("row", "col"), None), P("row", "col")),
        check_vma=False,
    )
```

```python
import functools

import jax
import jax.numpy as jnp
from jax import lax
from jax.experimental import pallas as pl
from jax.experimental.pallas import tpu as pltpu
from jax.sharding import PartitionSpec as P

MESH = pl.DeviceIdType.MESH
NN = (((1,), (0,)), ((), ()))
NT = (((1,), (1,)), ((), ()))
TN = (((0,), (0,)), ((), ()))
F32 = jnp.float32


def split(x):
    hi = x.astype(jnp.bfloat16)
    return hi, (x - hi.astype(F32)).astype(jnp.bfloat16)


def dot3(a, b, dims=NN):
    ah, al = a if isinstance(a, tuple) else split(a)
    bh, bl = b if isinstance(b, tuple) else split(b)
    d = functools.partial(lax.dot_general, dimension_numbers=dims, preferred_element_type=F32)
    return d(ah, bh) + (d(ah, bl) + d(al, bh))


PB = 32
HALF = 16


def panel_inverse(x, s):
    lane = lax.broadcasted_iota(jnp.int32, (8, 128), 1)
    sub = lax.broadcasted_iota(jnp.int32, (8, 128), 0)
    m = list(x)
    n = [jnp.where(lane == sub + (8 * g + PB * s), 1.0, 0.0).astype(F32) for g in range(4)]
    scale = [jnp.zeros((8, 128), F32) for _ in range(4)]
    coef = [jnp.zeros((8, 128), F32) for _ in range(4)]
    for q in range(2):
        c = {}
        for k in range(HALF):
            for g in range(2 * q, 4):
                at = PB * s + HALF * q + k
                c[k, g] = jnp.take_along_axis(m[g], lane * 0 + at, axis=1)
        for j in range(0, HALF, 2):
            gj = 2 * q + j // 8
            s0 = j % 8

            def row(v, i):
                return jnp.broadcast_to(v[i:i + 1, :], (8, 128))

            a = row(c[j, gj], s0)
            b = row(c[j, gj], s0 + 1)
            d = row(c[j + 1, gj], s0 + 1)
            det = a * d - b * b
            rdet = 1.0 / det
            ra = 1.0 / a
            scale[gj] = jnp.where(sub == s0, lax.rsqrt(a), jnp.where(sub == s0 + 1, lax.rsqrt(det * ra), scale[gj]))
            coef[gj] = jnp.where(sub == s0 + 1, b * ra, coef[gj])
            first = {k: row(c[k, gj], s0) for k in range(j + 2, HALF)}
            second = {k: row(c[k, gj], s0 + 1) for k in range(j + 2, HALF)}
            n0, n1 = row(n[gj], s0), row(n[gj], s0 + 1)
            m0, m1 = row(m[gj], s0), row(m[gj], s0 + 1)
            for g in range(gj, 4):
                if g == gj and s0 == 6:
                    continue
                e = d * c[j, g] - b * c[j + 1, g]
                f = a * c[j + 1, g] - b * c[j, g]
                if g == gj:
                    e = jnp.where(sub > s0 + 1, e, 0.0)
                    f = jnp.where(sub > s0 + 1, f, 0.0)
                e = e * rdet
                f = f * rdet
                for k in range(j + 2, HALF):
                    c[k, g] = c[k, g] - (e * first[k] + f * second[k])
                m[g] = m[g] - (e * m0 + f * m1)
                n[g] = n[g] - (e * n0 + f * n1)
    return [[(v[g] - coef[g] * pltpu.roll(v[g], 1, 0)) * scale[g] for g in range(4)] for v in (n, m)]


def chol_inverse(z_ref, between):
    here_lane = lax.broadcasted_iota(jnp.int32, (PB, 128), 1)
    for s in range(4):
        start = PB * s
        w, u = panel_inverse([z_ref[start + 8 * g:start + 8 * g + 8, :] for g in range(4)], s)
        here = here_lane // PB == s
        u = jnp.where(here, jnp.concatenate(w, axis=0), jnp.concatenate(u, axis=0))
        if s < 3:
            below = slice(start + PB, 128)
            lm = split(u.T[below])
            z_ref[below, :] = jnp.where(here_lane[:1] // PB == s, 0.0, z_ref[below, :]) - dot3(lm, split(u))
        z_ref[start:start + PB, :] = u
        between(s)


def lower(a):
    r = lax.broadcasted_iota(jnp.int32, a.shape, 0)
    c = lax.broadcasted_iota(jnp.int32, a.shape, 1)
    return jnp.where(c <= r, a, 0.0)


def nothing(s):
    pass


def schur(z_ref, w11, a21, a22):
    l21 = split(dot3(split(a21), w11, NT))
    z_ref[...] = a22 - dot3(l21, l21, NT)
    return -dot3(l21, w11)


def masked(a, rank, row0, col0):
    r = lax.broadcasted_iota(jnp.int32, a.shape, 0) + row0
    c = lax.broadcasted_iota(jnp.int32, a.shape, 1) + col0
    return jnp.where((r < rank) & (c < rank), a, jnp.where(r == c, 1.0, 0.0))


def row_masked(a, rank):
    return jnp.where(lax.broadcasted_iota(jnp.int32, a.shape, 0) < rank, a, 0.0)


def col_masked(a, rank):
    return jnp.where(lax.broadcasted_iota(jnp.int32, a.shape, 1) < rank, a, 0.0)


def far_first(i):
    return lax.rem(2 + 3 * i + 3 * lax.div(i * (i - 1), 2), 4)


AROUND = ((2, 2), (2, 1), (2, 3), (1, 2), (3, 2), (1, 1), (3, 3), (1, 3), (3, 1), (2, 0), (0, 2), (1, 0), (3, 0), (0, 1), (0, 3))
BY_SOURCE = ((2, 2), (2, 1), (2, 3), (2, 0), (1, 2), (3, 2), (1, 1), (3, 3), (1, 3), (3, 1), (1, 0), (3, 0), (0, 2), (0, 1), (0, 3))


def kernel(ranks, f_hbm, s_hbm, leaf, coupling, w11_out, pair, chain,
           fbuf, sbuf, sh, sl, part, xbuf, outbuf, rbuf, acc, samples, zb, wb, gb, cb, bth, btl, hown, hother,
           fsem, ssem, xs_sem, xr_sem, rs_sem, rr_sem, as_sem, ar_sem, ws_sem, wr_sem,
           zs_sem, zr_sem, vs_sem, vr_sem):
    z = lax.axis_index("row")
    me = lax.axis_index("col")
    core = lax.rem(me, 2)
    chip = lax.div(me, 2)
    x = lax.div(chip, 4)
    y = lax.rem(chip, 4)
    sibling = {"row": z, "col": chip * 2 + 1 - core}

    def chip_at(dx, dy):
        return lax.rem(x + dx, 4) * 4 + lax.rem(y + dy, 4)

    def peer(q):
        return {"row": z, "col": q * 2 + core}

    def along_z(step):
        return {"row": z + step * (1 - 2 * lax.rem(lax.div(z, step), 2)), "col": me}

    def chunk_copy(s):
        xs = lax.rem(x + far_first(s), 4)
        return pltpu.make_async_copy(f_hbm.at[pl.ds(pl.multiple_of(xs * 256, 256), 256)], fbuf.at[xs], fsem.at[s])

    def remote(src, dst, send, recv, device):
        return pltpu.make_async_remote_copy(src_ref=src, dst_ref=dst, send_sem=send, recv_sem=recv,
                                            device_id=device, device_id_type=MESH)

    scopy = pltpu.make_async_copy(s_hbm, sbuf, ssem)
    scopy.start()
    for s in range(4):
        chunk_copy(s).start()

    barrier = pltpu.get_barrier_semaphore()
    pl.semaphore_signal(barrier, inc=1, device_id=sibling, device_id_type=MESH)
    for dx, dy in AROUND:
        pl.semaphore_signal(barrier, inc=1, device_id=peer(chip_at(dx, dy)), device_id_type=MESH)
    for step in (1, 2):
        pl.semaphore_signal(barrier, inc=1, device_id=along_z(step), device_id_type=MESH)

    scopy.wait()
    sh[...], sl[...] = split(sbuf[...])

    def cores_copy(s):
        return remote(part.at[s, :, 1 - core], xbuf.at[s], xs_sem.at[s], xr_sem.at[s], sibling)

    def shard_copy(s, yy, q):
        return remote(outbuf.at[s, yy], rbuf.at[chip], rs_sem.at[q], rr_sem.at[chip], peer(q))

    @pl.loop(0, 5)
    def _(s):
        @pl.when(s < 4)
        def _():
            chunk_copy(s).wait()
            p = dot3(split(fbuf[lax.rem(x + far_first(s), 4)]), (sh[...], sl[...]))
            part[s] = p.reshape(4, 2, 32, 256)

            @pl.when(s == 0)
            def _():
                pl.semaphore_wait(barrier, 18)

            cores_copy(s).start()

        @pl.when(s > 0)
        def _():
            t = s - 1
            xt = lax.rem(x + far_first(t), 4)
            cores_copy(t).wait_recv()
            outbuf[t] = part[t, :, core] + xbuf[t]

            @pl.loop(0, 4)
            def _(u):
                yy = lax.rem(y + far_first(u), 4)
                q = xt * 4 + yy

                @pl.when(q != chip)
                def _():
                    shard_copy(t, yy, q).start()

    acc[...] = outbuf[3, y]
    for dx, dy in BY_SOURCE:
        q = chip_at(dx, dy)
        remote(outbuf.at[0, 0], rbuf.at[q], rs_sem.at[q], rr_sem.at[q], peer(q)).wait_recv()
        acc[...] += rbuf[q]

    chain[...] = acc[...]
    for h in range(2):
        samples[h, me] = acc[:, 128 * h:128 * h + 128]

    def own_copy(h, q):
        return remote(samples.at[h, me], samples.at[h, me], as_sem.at[h, q], ar_sem.at[h, chip], peer(q))

    def relay_copy(h, q):
        return remote(samples.at[h, q * 2 + core], samples.at[h, q * 2 + core], ws_sem.at[h, q], wr_sem.at[h, q], sibling)

    for h in range(2):
        for dx, dy in AROUND:
            own_copy(h, chip_at(dx, dy)).start()
        relay_copy(h, chip).start()

    def relay_half(h):
        for dx, dy in AROUND[::-1]:
            q = chip_at(dx, dy)
            remote(samples.at[h, me], samples.at[h, q * 2 + core], as_sem.at[h, q], ar_sem.at[h, q], peer(q)).wait_recv()
            relay_copy(h, q).start()

    def half_arrived(h):
        @pl.loop(0, 16)
        def _(q):
            remote(samples.at[h, q * 2 + core], samples.at[h, q * 2 + 1 - core], ws_sem.at[h, q], wr_sem.at[h, q],
                   sibling).wait_recv()

    def half_samples(h):
        return split(samples[h].reshape(1024, 128))

    def rows_of(piece, c):
        if piece == 0:
            return pl.ds(pl.multiple_of(c * 64, 64), 64)
        return pl.ds(pl.multiple_of(128 + c * 128, 128), 128)

    def z_copy(level, piece):
        at = rows_of(piece, core)
        i = level * 2 + piece
        return remote(hown.at[level, at], hother.at[level, at], zs_sem.at[i], zr_sem.at[i], along_z(level + 1))

    def z_direct():
        at = pl.ds(0, 128)
        return remote(hown.at[0, at], hother.at[0, at], zs_sem.at[0], zr_sem.at[0], along_z(1))

    def z_relay(level, piece, c):
        at = rows_of(piece, c)
        i = level * 2 + piece
        return remote(hother.at[level, at], hother.at[level, at], vs_sem.at[i], vr_sem.at[i], sibling)

    relay_half(0)
    half_arrived(0)
    first = half_samples(0)
    pair[0] = dot3(first, first, TN)

    def coupling_tile(i):
        cols = pl.ds(pl.multiple_of(i * 256, 256), 256)
        f = fbuf[:, :, cols].reshape(1024, 256)
        coupling[:, cols] = dot3((bth[...], btl[...]), split(f))

    @pl.loop(0, 3)
    def _(level):
        rank = ranks[level, z]
        zb[...] = masked(pair[0], rank, 0, 0)

        def between(s):
            if s == 1:
                @pl.when(level == 0)
                def _():
                    relay_half(1)

                @pl.when(level > 0)
                def _():
                    z_copy(level - 1, 1).wait_recv()
                    z_relay(level - 1, 1, core).start()

        chol_inverse(zb, between)
        w11_out[...] = lower(zb[...])

        @pl.when(level == 0)
        def _():
            half_arrived(1)
            left, right = half_samples(0), half_samples(1)
            pair[1] = dot3(right, left, TN)
            pair[2] = dot3(right, right, TN)

        @pl.when(level > 0)
        def _():
            z_relay(level - 1, 1, 1 - core).wait_recv()
            pair[1] += hother[level - 1, 128:256]
            pair[2] += hother[level - 1, 256:384]
            z_copy(level - 1, 1).wait_send()
            z_relay(level - 1, 1, core).wait_send()

        @pl.when(level < 2)
        def _():
            w11 = w11_out[...]
            m21 = schur(zb, split(w11), masked(pair[1], rank, 128, 0), masked(pair[2], rank, 128, 128))
            gb[:128, :128] = pair[0]
            gb[:128, 128:] = pair[1].T
            gb[128:, :128] = pair[1]
            gb[128:, 128:] = pair[2]
            chol_inverse(zb, nothing)
            w22 = lower(zb[...])
            wb[:128, :128] = w11
            wb[:128, 128:] = jnp.zeros((128, 128), F32)
            wb[128:, :128] = dot3(w22, m21)
            wb[128:, 128:] = w22
            w = split(wb[...])
            g = gb[...]
            c = split(dot3(w, split(row_masked(g, rank))))
            ct = split(dot3(split(col_masked(g, rank)), w, NT))

            def block(i, j):
                a, b = slice(128 * i, 128 * i + 128), slice(128 * j, 128 * j + 128)
                return dot3((ct[0][a], ct[1][a]), (c[0][:, b], c[1][:, b]))

            h11 = block(0, 0)
            hown[level, 0:128] = h11

            @pl.when(level == 0)
            def _():
                z_direct().start()

            @pl.when(level == 1)
            def _():
                z_copy(1, 0).start()

            h21, h22 = block(1, 0), block(1, 1)
            hown[level, 128:256] = h21
            hown[level, 256:384] = h22
            z_copy(level, 1).start()
            pair[0] = h11
            pair[1] = h21
            pair[2] = h22
            cb[0] = c[0]
            cb[1] = c[1]
            moved = dot3(split(col_masked(chain[...], rank)), w, NT)
            chain[...] = moved

            @pl.when(level == 0)
            def _():
                leaf[...] = chain[...]
                w0 = split(wb[...])
                whole = col_masked(jnp.concatenate([samples[0].reshape(1024, 128), samples[1].reshape(1024, 128)], axis=1), rank)
                bth[...], btl[...] = split(dot3(w0, split(whole), NT))

            @pl.loop(0, 4)
            def _(i):
                coupling_tile(level * 4 + i)

            chain[...] = dot3(split(chain[...]), (cb[0], cb[1]))

            @pl.when(level == 0)
            def _():
                z_direct().wait()

            @pl.when(level == 1)
            def _():
                z_copy(1, 0).wait()
                relay = z_relay(1, 0, core)
                relay.start()
                z_relay(1, 0, 1 - core).wait_recv()
                relay.wait_send()

            pair[0] += hother[level, 0:128]

    for s in range(4):
        cores_copy(s).wait_send()
    for dx, dy in AROUND:
        q = chip_at(dx, dy)
        shard_copy(0, 0, q).wait_send()
        own_copy(0, q).wait_send()
        own_copy(1, q).wait_send()

    @pl.loop(0, 16)
    def _(q):
        relay_copy(0, q).wait_send()
        relay_copy(1, q).wait_send()


def last_kernel(ranks, leaf_in, coupling_in, w11, pair, chain, leaf, top, coupling, zb, sem):
    copies = [pltpu.make_async_copy(coupling_in, coupling, sem.at[0]), pltpu.make_async_copy(leaf_in, leaf, sem.at[1])]
    for copy in copies:
        copy.start()
    rank = ranks[2, lax.axis_index("row")]
    w = split(w11[...])
    m21 = split(schur(zb, w, masked(pair[1], rank, 128, 0), masked(pair[2], rank, 128, 128)))
    t = col_masked(chain[...], rank)
    left = split(t[:, :128])
    right = t[:, 128:] + dot3(left, m21, NT)
    chol_inverse(zb, nothing)
    top[:, :128] = dot3(left, w, NT)
    top[:, 128:] = dot3(split(right), split(lower(zb[...])), NT)
    for copy in copies:
        copy.wait()


def body(frontal, sketch, rank_table):
    vmem = pl.BlockSpec(memory_space=pltpu.VMEM)
    hbm = pl.BlockSpec(memory_space=pltpu.HBM)
    dma = pltpu.SemaphoreType.DMA
    bf16 = jnp.bfloat16
    smem = pl.BlockSpec(memory_space=pltpu.SMEM)
    frontal = pltpu.with_memory_space_constraint(frontal, pltpu.HBM)
    sketch = pltpu.with_memory_space_constraint(sketch, pltpu.HBM)
    rank_table = pltpu.with_memory_space_constraint(rank_table, pltpu.HBM)
    held = pl.pallas_call(
        kernel,
        out_shape=(pltpu.VMEM((32, 256), F32), pltpu.VMEM((256, 2048), F32), pltpu.VMEM((128, 128), F32),
                   pltpu.VMEM((3, 128, 128), F32), pltpu.VMEM((32, 256), F32)),
        in_specs=[smem, hbm, hbm],
        out_specs=(vmem,) * 5,
        scratch_shapes=[
            pltpu.VMEM((4, 256, 2048), F32),
            pltpu.VMEM((2048, 256), F32),
            pltpu.VMEM((2048, 256), bf16),
            pltpu.VMEM((2048, 256), bf16),
            pltpu.VMEM((4, 4, 2, 32, 256), F32),
            pltpu.VMEM((4, 4, 32, 256), F32),
            pltpu.VMEM((4, 4, 32, 256), F32),
            pltpu.VMEM((16, 32, 256), F32),
            pltpu.VMEM((32, 256), F32),
            pltpu.VMEM((2, 32, 32, 128), F32),
            pltpu.VMEM((128, 128), F32),
            pltpu.VMEM((256, 256), F32),
            pltpu.VMEM((256, 256), F32),
            pltpu.VMEM((2, 256, 256), bf16),
            pltpu.VMEM((256, 1024), bf16),
            pltpu.VMEM((256, 1024), bf16),
            pltpu.VMEM((2, 384, 128), F32),
            pltpu.VMEM((2, 384, 128), F32),
            dma((4,)), dma, dma((4,)), dma((4,)),
            dma((16,)), dma((16,)), dma((2, 16)), dma((2, 16)), dma((2, 16)), dma((2, 16)),
            dma((4,)), dma((4,)), dma((4,)), dma((4,)),
        ],
        compiler_params=pltpu.CompilerParams(collective_id=0, has_side_effects=True, vmem_limit_bytes=40 * 2**20),
        cost_estimate=pl.CostEstimate(flops=7 * 2**30, bytes_accessed=12 * 2**20, transcendentals=0),
    )(rank_table, frontal, sketch)
    return pl.pallas_call(
        last_kernel,
        out_shape=(jax.ShapeDtypeStruct((32, 256), F32), jax.ShapeDtypeStruct((32, 256), F32),
                   jax.ShapeDtypeStruct((256, 2048), F32)),
        in_specs=[smem] + [vmem] * 5,
        out_specs=(hbm, vmem, hbm),
        scratch_shapes=[pltpu.VMEM((128, 128), F32), dma((2,))],
        compiler_params=pltpu.CompilerParams(vmem_limit_bytes=16 * 2**20),
    )(rank_table, *held)


def solution(mesh):
    return jax.shard_map(
        body,
        mesh=mesh,
        in_specs=(P("row", "col"), P("col", None), P()),
        out_specs=(P(("row", "col"), None), P(("row", "col"), None), P("row", "col")),
        check_vma=False,
    )
```

```python
import functools

import jax
import jax.numpy as jnp
from jax import lax
from jax.experimental import pallas as pl
from jax.experimental.pallas import tpu as pltpu
from jax.sharding import PartitionSpec as P

MESH = pl.DeviceIdType.MESH
NN = (((1,), (0,)), ((), ()))
NT = (((1,), (1,)), ((), ()))
TN = (((0,), (0,)), ((), ()))
F32 = jnp.float32


def split(x):
    hi = x.astype(jnp.bfloat16)
    return hi, (x - hi.astype(F32)).astype(jnp.bfloat16)


def dot3(a, b, dims=NN):
    ah, al = a if isinstance(a, tuple) else split(a)
    bh, bl = b if isinstance(b, tuple) else split(b)
    d = functools.partial(lax.dot_general, dimension_numbers=dims, preferred_element_type=F32)
    return d(ah, bh) + (d(ah, bl) + d(al, bh))


PB = 32
HALF = 16


def panel_inverse(x, s):
    lane = lax.broadcasted_iota(jnp.int32, (8, 128), 1)
    sub = lax.broadcasted_iota(jnp.int32, (8, 128), 0)
    m = list(x)
    n = [jnp.where(lane == sub + (8 * g + PB * s), 1.0, 0.0).astype(F32) for g in range(4)]
    scale = [jnp.zeros((8, 128), F32) for _ in range(4)]
    coef = [jnp.zeros((8, 128), F32) for _ in range(4)]
    for q in range(2):
        c = {}
        for k in range(HALF):
            for g in range(2 * q, 4):
                at = PB * s + HALF * q + k
                c[k, g] = jnp.take_along_axis(m[g], lane * 0 + at, axis=1)
        for j in range(0, HALF, 2):
            gj = 2 * q + j // 8
            s0 = j % 8

            def row(v, i):
                return jnp.broadcast_to(v[i:i + 1, :], (8, 128))

            a = row(c[j, gj], s0)
            b = row(c[j, gj], s0 + 1)
            d = row(c[j + 1, gj], s0 + 1)
            det = a * d - b * b
            rdet = 1.0 / det
            ra = 1.0 / a
            scale[gj] = jnp.where(sub == s0, lax.rsqrt(a), jnp.where(sub == s0 + 1, lax.rsqrt(det * ra), scale[gj]))
            coef[gj] = jnp.where(sub == s0 + 1, b * ra, coef[gj])
            first = {k: row(c[k, gj], s0) for k in range(j + 2, HALF)}
            second = {k: row(c[k, gj], s0 + 1) for k in range(j + 2, HALF)}
            n0, n1 = row(n[gj], s0), row(n[gj], s0 + 1)
            m0, m1 = row(m[gj], s0), row(m[gj], s0 + 1)
            for g in range(gj, 4):
                if g == gj and s0 == 6:
                    continue
                e = d * c[j, g] - b * c[j + 1, g]
                f = a * c[j + 1, g] - b * c[j, g]
                if g == gj:
                    e = jnp.where(sub > s0 + 1, e, 0.0)
                    f = jnp.where(sub > s0 + 1, f, 0.0)
                e = e * rdet
                f = f * rdet
                for k in range(j + 2, HALF):
                    c[k, g] = c[k, g] - (e * first[k] + f * second[k])
                m[g] = m[g] - (e * m0 + f * m1)
                n[g] = n[g] - (e * n0 + f * n1)
    return [[(v[g] - coef[g] * pltpu.roll(v[g], 1, 0)) * scale[g] for g in range(4)] for v in (n, m)]


def chol_inverse(z_ref, between):
    here_lane = lax.broadcasted_iota(jnp.int32, (PB, 128), 1)
    for s in range(4):
        start = PB * s
        w, u = panel_inverse([z_ref[start + 8 * g:start + 8 * g + 8, :] for g in range(4)], s)
        here = here_lane // PB == s
        u = jnp.where(here, jnp.concatenate(w, axis=0), jnp.concatenate(u, axis=0))
        if s < 3:
            below = slice(start + PB, 128)
            lm = split(u.T[below])
            z_ref[below, :] = jnp.where(here_lane[:1] // PB == s, 0.0, z_ref[below, :]) - dot3(lm, split(u))
        z_ref[start:start + PB, :] = u
        between(s)


def lower(a):
    r = lax.broadcasted_iota(jnp.int32, a.shape, 0)
    c = lax.broadcasted_iota(jnp.int32, a.shape, 1)
    return jnp.where(c <= r, a, 0.0)


def nothing(s):
    pass


def schur(z_ref, w11, a21, a22):
    l21 = split(dot3(split(a21), w11, NT))
    z_ref[...] = a22 - dot3(l21, l21, NT)
    return -dot3(l21, w11)


def masked(a, rank, row0, col0):
    r = lax.broadcasted_iota(jnp.int32, a.shape, 0) + row0
    c = lax.broadcasted_iota(jnp.int32, a.shape, 1) + col0
    return jnp.where((r < rank) & (c < rank), a, jnp.where(r == c, 1.0, 0.0))


def row_masked(a, rank):
    return jnp.where(lax.broadcasted_iota(jnp.int32, a.shape, 0) < rank, a, 0.0)


def col_masked(a, rank):
    return jnp.where(lax.broadcasted_iota(jnp.int32, a.shape, 1) < rank, a, 0.0)


def far_first(i):
    return lax.rem(2 + 3 * i + 3 * lax.div(i * (i - 1), 2), 4)


AROUND = ((2, 2), (2, 1), (2, 3), (1, 2), (3, 2), (1, 1), (3, 3), (1, 3), (3, 1), (2, 0), (0, 2), (1, 0), (3, 0), (0, 1), (0, 3))
BY_SOURCE = ((2, 2), (2, 1), (2, 3), (2, 0), (1, 2), (3, 2), (1, 1), (3, 3), (1, 3), (3, 1), (1, 0), (3, 0), (0, 2), (0, 1), (0, 3))


def kernel(ranks, f_hbm, s_hbm, leaf, coupling, w11_out, pair, chain,
           fbuf, sbuf, sh, sl, part, xbuf, outbuf, rbuf, acc, samples, zb, wb, gb, hb, cb, bth, btl, hown, hother,
           fsem, ssem, xs_sem, xr_sem, rs_sem, rr_sem, as_sem, ar_sem, ws_sem, wr_sem,
           zs_sem, zr_sem, vs_sem, vr_sem):
    z = lax.axis_index("row")
    me = lax.axis_index("col")
    core = lax.rem(me, 2)
    chip = lax.div(me, 2)
    x = lax.div(chip, 4)
    y = lax.rem(chip, 4)
    sibling = {"row": z, "col": chip * 2 + 1 - core}

    def chip_at(dx, dy):
        return lax.rem(x + dx, 4) * 4 + lax.rem(y + dy, 4)

    def peer(q):
        return {"row": z, "col": q * 2 + core}

    def along_z(step):
        return {"row": z + step * (1 - 2 * lax.rem(lax.div(z, step), 2)), "col": me}

    def chunk_copy(s):
        xs = lax.rem(x + far_first(s), 4)
        return pltpu.make_async_copy(f_hbm.at[pl.ds(pl.multiple_of(xs * 256, 256), 256)], fbuf.at[xs], fsem.at[s])

    def remote(src, dst, send, recv, device):
        return pltpu.make_async_remote_copy(src_ref=src, dst_ref=dst, send_sem=send, recv_sem=recv,
                                            device_id=device, device_id_type=MESH)

    scopy = pltpu.make_async_copy(s_hbm, sbuf, ssem)
    scopy.start()
    for s in range(4):
        chunk_copy(s).start()

    barrier = pltpu.get_barrier_semaphore()
    pl.semaphore_signal(barrier, inc=1, device_id=sibling, device_id_type=MESH)
    for dx, dy in AROUND:
        pl.semaphore_signal(barrier, inc=1, device_id=peer(chip_at(dx, dy)), device_id_type=MESH)
    for step in (1, 2):
        pl.semaphore_signal(barrier, inc=1, device_id=along_z(step), device_id_type=MESH)

    scopy.wait()
    sh[...], sl[...] = split(sbuf[...])

    def cores_copy(s):
        return remote(part.at[s, :, 1 - core], xbuf.at[s], xs_sem.at[s], xr_sem.at[s], sibling)

    def shard_copy(s, yy, q):
        return remote(outbuf.at[s, yy], rbuf.at[chip], rs_sem.at[q], rr_sem.at[chip], peer(q))

    @pl.loop(0, 5)
    def _(s):
        @pl.when(s < 4)
        def _():
            chunk_copy(s).wait()
            p = dot3(split(fbuf[lax.rem(x + far_first(s), 4)]), (sh[...], sl[...]))
            part[s] = p.reshape(4, 2, 32, 256)

            @pl.when(s == 0)
            def _():
                pl.semaphore_wait(barrier, 18)

            cores_copy(s).start()

        @pl.when(s > 0)
        def _():
            t = s - 1
            xt = lax.rem(x + far_first(t), 4)
            cores_copy(t).wait_recv()
            outbuf[t] = part[t, :, core] + xbuf[t]

            @pl.loop(0, 4)
            def _(u):
                yy = lax.rem(y + far_first(u), 4)
                q = xt * 4 + yy

                @pl.when(q != chip)
                def _():
                    shard_copy(t, yy, q).start()

    acc[...] = outbuf[3, y]
    for dx, dy in BY_SOURCE:
        q = chip_at(dx, dy)
        remote(outbuf.at[0, 0], rbuf.at[q], rs_sem.at[q], rr_sem.at[q], peer(q)).wait_recv()
        acc[...] += rbuf[q]

    chain[...] = acc[...]
    for h in range(2):
        samples[h, me] = acc[:, 128 * h:128 * h + 128]

    def own_copy(h, q):
        return remote(samples.at[h, me], samples.at[h, me], as_sem.at[h, q], ar_sem.at[h, chip], peer(q))

    def relay_copy(h, q):
        return remote(samples.at[h, q * 2 + core], samples.at[h, q * 2 + core], ws_sem.at[h, q], wr_sem.at[h, q], sibling)

    for h in range(2):
        for dx, dy in AROUND:
            own_copy(h, chip_at(dx, dy)).start()
        relay_copy(h, chip).start()

    def relay_half(h):
        for dx, dy in AROUND[::-1]:
            q = chip_at(dx, dy)
            remote(samples.at[h, me], samples.at[h, q * 2 + core], as_sem.at[h, q], ar_sem.at[h, q], peer(q)).wait_recv()
            relay_copy(h, q).start()

    def half_arrived(h):
        @pl.loop(0, 16)
        def _(q):
            remote(samples.at[h, q * 2 + core], samples.at[h, q * 2 + 1 - core], ws_sem.at[h, q], wr_sem.at[h, q],
                   sibling).wait_recv()

    def half_samples(h):
        return split(samples[h].reshape(1024, 128))

    def rows_of(piece, c):
        if piece == 0:
            return pl.ds(pl.multiple_of(c * 64, 64), 64)
        return pl.ds(pl.multiple_of(128 + c * 128, 128), 128)

    def z_copy(level, piece):
        at = rows_of(piece, core)
        i = level * 2 + piece
        return remote(hown.at[level, at], hother.at[level, at], zs_sem.at[i], zr_sem.at[i], along_z(level + 1))

    def z_direct():
        at = pl.ds(0, 128)
        return remote(hown.at[0, at], hother.at[0, at], zs_sem.at[0], zr_sem.at[0], along_z(1))

    def z_relay(level, piece, c):
        at = rows_of(piece, c)
        i = level * 2 + piece
        return remote(hother.at[level, at], hother.at[level, at], vs_sem.at[i], vr_sem.at[i], sibling)

    relay_half(0)
    half_arrived(0)
    first = half_samples(0)
    pair[0] = dot3(first, first, TN)

    def coupling_tile(i):
        cols = pl.ds(pl.multiple_of(i * 256, 256), 256)
        f = fbuf[:, :, cols].reshape(1024, 256)
        coupling[:, cols] = dot3((bth[...], btl[...]), split(f))

    @pl.loop(0, 3)
    def _(level):
        rank = ranks[level, z]
        zb[...] = masked(pair[0], rank, 0, 0)

        def between(s):
            if s == 1:
                @pl.when(level == 0)
                def _():
                    relay_half(1)

                @pl.when(level > 0)
                def _():
                    z_copy(level - 1, 1).wait_recv()
                    z_relay(level - 1, 1, core).start()

        chol_inverse(zb, between)
        w11_out[...] = lower(zb[...])

        @pl.when(level == 0)
        def _():
            half_arrived(1)
            left, right = half_samples(0), half_samples(1)
            pair[1] = dot3(right, left, TN)
            pair[2] = dot3(right, right, TN)

        @pl.when(level > 0)
        def _():
            z_relay(level - 1, 1, 1 - core).wait_recv()
            pair[1] += hother[level - 1, 128:256]
            pair[2] += hother[level - 1, 256:384]
            z_copy(level - 1, 1).wait_send()
            z_relay(level - 1, 1, core).wait_send()

        @pl.when(level < 2)
        def _():
            w11 = w11_out[...]
            m21 = schur(zb, split(w11), masked(pair[1], rank, 128, 0), masked(pair[2], rank, 128, 128))
            gb[:128, :128] = pair[0]
            gb[:128, 128:] = pair[1].T
            gb[128:, :128] = pair[1]
            gb[128:, 128:] = pair[2]
            g = gb[...]
            gr = row_masked(g, rank)
            gc = col_masked(g, rank)
            w1, m2 = split(w11), split(m21)
            gr1, gc1 = split(gr[:128]), split(gc[:, :128])
            c1 = split(dot3(w1, gr1))
            ct1 = split(dot3(gc1, w1, NT))
            r2 = split(gr[128:] + dot3(m2, gr1))
            rt2 = split(gc[:, 128:] + dot3(gc1, m2, NT))
            hb[...] = dot3(ct1, c1)
            chol_inverse(zb, nothing)
            w22 = lower(zb[...])
            w2 = split(w22)
            c2 = split(dot3(w2, r2))
            ct2 = split(dot3(rt2, w2, NT))

            def block(i, j):
                a, b = slice(128 * i, 128 * i + 128), slice(128 * j, 128 * j + 128)
                return hb[a, b] + dot3((ct2[0][a], ct2[1][a]), (c2[0][:, b], c2[1][:, b]))

            h11 = block(0, 0)
            hown[level, 0:128] = h11

            @pl.when(level == 0)
            def _():
                z_direct().start()

            @pl.when(level == 1)
            def _():
                z_copy(1, 0).start()

            h21, h22 = block(1, 0), block(1, 1)
            hown[level, 128:256] = h21
            hown[level, 256:384] = h22
            z_copy(level, 1).start()
            pair[0] = h11
            pair[1] = h21
            pair[2] = h22
            for i in range(2):
                cb[i, :128] = c1[i]
                cb[i, 128:] = c2[i]
            wb[:128, :128] = w11
            wb[:128, 128:] = jnp.zeros((128, 128), F32)
            wb[128:, :128] = dot3(w2, m2)
            wb[128:, 128:] = w22
            chain[...] = dot3(split(col_masked(chain[...], rank)), split(wb[...]), NT)

            @pl.when(level == 0)
            def _():
                leaf[...] = chain[...]
                w0 = split(wb[...])
                whole = col_masked(jnp.concatenate([samples[0].reshape(1024, 128), samples[1].reshape(1024, 128)], axis=1), rank)
                bth[...], btl[...] = split(dot3(w0, split(whole), NT))

            @pl.loop(0, 3)
            def _(i):
                coupling_tile(level * 3 + i)

            @pl.when(level == 1)
            def _():
                @pl.loop(6, 8)
                def _(i):
                    coupling_tile(i)

            chain[...] = dot3(split(chain[...]), (cb[0], cb[1]))

            @pl.when(level == 0)
            def _():
                z_direct().wait()

            @pl.when(level == 1)
            def _():
                z_copy(1, 0).wait()
                relay = z_relay(1, 0, core)
                relay.start()
                z_relay(1, 0, 1 - core).wait_recv()
                relay.wait_send()

            pair[0] += hother[level, 0:128]

    for s in range(4):
        cores_copy(s).wait_send()
    for dx, dy in AROUND:
        q = chip_at(dx, dy)
        shard_copy(0, 0, q).wait_send()
        own_copy(0, q).wait_send()
        own_copy(1, q).wait_send()

    @pl.loop(0, 16)
    def _(q):
        relay_copy(0, q).wait_send()
        relay_copy(1, q).wait_send()


def last_kernel(ranks, leaf_in, coupling_in, w11, pair, chain, leaf, top, coupling, zb, sem):
    copies = [pltpu.make_async_copy(coupling_in, coupling, sem.at[0]), pltpu.make_async_copy(leaf_in, leaf, sem.at[1])]
    for copy in copies:
        copy.start()
    rank = ranks[2, lax.axis_index("row")]
    w = split(w11[...])
    m21 = split(schur(zb, w, masked(pair[1], rank, 128, 0), masked(pair[2], rank, 128, 128)))
    t = col_masked(chain[...], rank)
    left = split(t[:, :128])
    right = t[:, 128:] + dot3(left, m21, NT)
    chol_inverse(zb, nothing)
    top[:, :128] = dot3(left, w, NT)
    top[:, 128:] = dot3(split(right), split(lower(zb[...])), NT)
    for copy in copies:
        copy.wait()


def body(frontal, sketch, rank_table):
    vmem = pl.BlockSpec(memory_space=pltpu.VMEM)
    hbm = pl.BlockSpec(memory_space=pltpu.HBM)
    dma = pltpu.SemaphoreType.DMA
    bf16 = jnp.bfloat16
    smem = pl.BlockSpec(memory_space=pltpu.SMEM)
    frontal = pltpu.with_memory_space_constraint(frontal, pltpu.HBM)
    sketch = pltpu.with_memory_space_constraint(sketch, pltpu.HBM)
    rank_table = pltpu.with_memory_space_constraint(rank_table, pltpu.HBM)
    held = pl.pallas_call(
        kernel,
        out_shape=(pltpu.VMEM((32, 256), F32), pltpu.VMEM((256, 2048), F32), pltpu.VMEM((128, 128), F32),
                   pltpu.VMEM((3, 128, 128), F32), pltpu.VMEM((32, 256), F32)),
        in_specs=[smem, hbm, hbm],
        out_specs=(vmem,) * 5,
        scratch_shapes=[
            pltpu.VMEM((4, 256, 2048), F32),
            pltpu.VMEM((2048, 256), F32),
            pltpu.VMEM((2048, 256), bf16),
            pltpu.VMEM((2048, 256), bf16),
            pltpu.VMEM((4, 4, 2, 32, 256), F32),
            pltpu.VMEM((4, 4, 32, 256), F32),
            pltpu.VMEM((4, 4, 32, 256), F32),
            pltpu.VMEM((16, 32, 256), F32),
            pltpu.VMEM((32, 256), F32),
            pltpu.VMEM((2, 32, 32, 128), F32),
            pltpu.VMEM((128, 128), F32),
            pltpu.VMEM((256, 256), F32),
            pltpu.VMEM((256, 256), F32),
            pltpu.VMEM((256, 256), F32),
            pltpu.VMEM((2, 256, 256), bf16),
            pltpu.VMEM((256, 1024), bf16),
            pltpu.VMEM((256, 1024), bf16),
            pltpu.VMEM((2, 384, 128), F32),
            pltpu.VMEM((2, 384, 128), F32),
            dma((4,)), dma, dma((4,)), dma((4,)),
            dma((16,)), dma((16,)), dma((2, 16)), dma((2, 16)), dma((2, 16)), dma((2, 16)),
            dma((4,)), dma((4,)), dma((4,)), dma((4,)),
        ],
        compiler_params=pltpu.CompilerParams(collective_id=0, has_side_effects=True, vmem_limit_bytes=40 * 2**20),
        cost_estimate=pl.CostEstimate(flops=7 * 2**30, bytes_accessed=12 * 2**20, transcendentals=0),
    )(rank_table, frontal, sketch)
    return pl.pallas_call(
        last_kernel,
        out_shape=(jax.ShapeDtypeStruct((32, 256), F32), jax.ShapeDtypeStruct((32, 256), F32),
                   jax.ShapeDtypeStruct((256, 2048), F32)),
        in_specs=[smem] + [vmem] * 5,
        out_specs=(hbm, vmem, hbm),
        scratch_shapes=[pltpu.VMEM((128, 128), F32), dma((2,))],
        compiler_params=pltpu.CompilerParams(vmem_limit_bytes=16 * 2**20),
    )(rank_table, *held)


def solution(mesh):
    return jax.shard_map(
        body,
        mesh=mesh,
        in_specs=(P("row", "col"), P("col", None), P()),
        out_specs=(P(("row", "col"), None), P(("row", "col"), None), P("row", "col")),
        check_vma=False,
    )
```

```python
import functools

import jax
import jax.numpy as jnp
from jax import lax
from jax.experimental import pallas as pl
from jax.experimental.pallas import tpu as pltpu
from jax.sharding import PartitionSpec as P

MESH = pl.DeviceIdType.MESH
NN = (((1,), (0,)), ((), ()))
NT = (((1,), (1,)), ((), ()))
TN = (((0,), (0,)), ((), ()))
F32 = jnp.float32


def split(x):
    hi = x.astype(jnp.bfloat16)
    return hi, (x - hi.astype(F32)).astype(jnp.bfloat16)


def dot3(a, b, dims=NN):
    ah, al = a if isinstance(a, tuple) else split(a)
    bh, bl = b if isinstance(b, tuple) else split(b)
    d = functools.partial(lax.dot_general, dimension_numbers=dims, preferred_element_type=F32)
    return d(ah, bh) + (d(ah, bl) + d(al, bh))


PB = 32
HALF = 16


def panel_inverse(x, s):
    lane = lax.broadcasted_iota(jnp.int32, (8, 128), 1)
    sub = lax.broadcasted_iota(jnp.int32, (8, 128), 0)
    m = list(x)
    n = [jnp.where(lane == sub + (8 * g + PB * s), 1.0, 0.0).astype(F32) for g in range(4)]
    scale = [jnp.zeros((8, 128), F32) for _ in range(4)]
    coef = [jnp.zeros((8, 128), F32) for _ in range(4)]
    for q in range(2):
        c = {}
        for k in range(HALF):
            for g in range(2 * q, 4):
                at = PB * s + HALF * q + k
                c[k, g] = jnp.take_along_axis(m[g], lane * 0 + at, axis=1)
        for j in range(0, HALF, 2):
            gj = 2 * q + j // 8
            s0 = j % 8

            def row(v, i):
                return jnp.broadcast_to(v[i:i + 1, :], (8, 128))

            a = row(c[j, gj], s0)
            b = row(c[j, gj], s0 + 1)
            d = row(c[j + 1, gj], s0 + 1)
            det = a * d - b * b
            rdet = 1.0 / det
            ra = 1.0 / a
            scale[gj] = jnp.where(sub == s0, lax.rsqrt(a), jnp.where(sub == s0 + 1, lax.rsqrt(det * ra), scale[gj]))
            coef[gj] = jnp.where(sub == s0 + 1, b * ra, coef[gj])
            first = {k: row(c[k, gj], s0) for k in range(j + 2, HALF)}
            second = {k: row(c[k, gj], s0 + 1) for k in range(j + 2, HALF)}
            n0, n1 = row(n[gj], s0), row(n[gj], s0 + 1)
            m0, m1 = row(m[gj], s0), row(m[gj], s0 + 1)
            for g in range(gj, 4):
                if g == gj and s0 == 6:
                    continue
                e = d * c[j, g] - b * c[j + 1, g]
                f = a * c[j + 1, g] - b * c[j, g]
                if g == gj:
                    e = jnp.where(sub > s0 + 1, e, 0.0)
                    f = jnp.where(sub > s0 + 1, f, 0.0)
                e = e * rdet
                f = f * rdet
                for k in range(j + 2, HALF):
                    c[k, g] = c[k, g] - (e * first[k] + f * second[k])
                m[g] = m[g] - (e * m0 + f * m1)
                n[g] = n[g] - (e * n0 + f * n1)
    return [[(v[g] - coef[g] * pltpu.roll(v[g], 1, 0)) * scale[g] for g in range(4)] for v in (n, m)]


def chol_inverse(z_ref, between):
    here_lane = lax.broadcasted_iota(jnp.int32, (PB, 128), 1)
    for s in range(4):
        start = PB * s
        w, u = panel_inverse([z_ref[start + 8 * g:start + 8 * g + 8, :] for g in range(4)], s)
        here = here_lane // PB == s
        u = jnp.where(here, jnp.concatenate(w, axis=0), jnp.concatenate(u, axis=0))
        if s < 3:
            below = slice(start + PB, 128)
            lm = split(u.T[below])
            z_ref[below, :] = jnp.where(here_lane[:1] // PB == s, 0.0, z_ref[below, :]) - dot3(lm, split(u))
        z_ref[start:start + PB, :] = u
        between(s)


def lower(a):
    r = lax.broadcasted_iota(jnp.int32, a.shape, 0)
    c = lax.broadcasted_iota(jnp.int32, a.shape, 1)
    return jnp.where(c <= r, a, 0.0)


def nothing(s):
    pass


def schur(z_ref, w11, a21, a22):
    l21 = split(dot3(split(a21), w11, NT))
    z_ref[...] = a22 - dot3(l21, l21, NT)
    return -dot3(l21, w11)


def masked(a, rank, row0, col0):
    r = lax.broadcasted_iota(jnp.int32, a.shape, 0) + row0
    c = lax.broadcasted_iota(jnp.int32, a.shape, 1) + col0
    return jnp.where((r < rank) & (c < rank), a, jnp.where(r == c, 1.0, 0.0))


def row_masked(a, rank):
    return jnp.where(lax.broadcasted_iota(jnp.int32, a.shape, 0) < rank, a, 0.0)


def col_masked(a, rank):
    return jnp.where(lax.broadcasted_iota(jnp.int32, a.shape, 1) < rank, a, 0.0)


def far_first(i):
    return lax.rem(2 + 3 * i + 3 * lax.div(i * (i - 1), 2), 4)


AROUND = ((2, 2), (2, 1), (2, 3), (1, 2), (3, 2), (1, 1), (3, 3), (1, 3), (3, 1), (2, 0), (0, 2), (1, 0), (3, 0), (0, 1), (0, 3))
BY_SOURCE = ((2, 2), (2, 1), (2, 3), (2, 0), (1, 2), (3, 2), (1, 1), (3, 3), (1, 3), (3, 1), (1, 0), (3, 0), (0, 2), (0, 1), (0, 3))


def kernel(ranks, f_hbm, s_hbm, leaf, coupling, w11_out, pair, chain,
           fbuf, sbuf, sh, sl, part, xbuf, outbuf, rbuf, acc, samples, zb, wb, gb, hb, cb, bth, btl, hown, hother,
           fsem, ssem, xs_sem, xr_sem, rs_sem, rr_sem, as_sem, ar_sem, ws_sem, wr_sem,
           zs_sem, zr_sem, vs_sem, vr_sem):
    z = lax.axis_index("row")
    me = lax.axis_index("col")
    core = lax.rem(me, 2)
    chip = lax.div(me, 2)
    x = lax.div(chip, 4)
    y = lax.rem(chip, 4)
    sibling = {"row": z, "col": chip * 2 + 1 - core}

    def chip_at(dx, dy):
        return lax.rem(x + dx, 4) * 4 + lax.rem(y + dy, 4)

    def peer(q):
        return {"row": z, "col": q * 2 + core}

    def along_z(step):
        return {"row": z + step * (1 - 2 * lax.rem(lax.div(z, step), 2)), "col": me}

    def chunk_copy(s):
        xs = lax.rem(x + far_first(s), 4)
        return pltpu.make_async_copy(f_hbm.at[pl.ds(pl.multiple_of(xs * 256, 256), 256)], fbuf.at[xs], fsem.at[s])

    def remote(src, dst, send, recv, device):
        return pltpu.make_async_remote_copy(src_ref=src, dst_ref=dst, send_sem=send, recv_sem=recv,
                                            device_id=device, device_id_type=MESH)

    scopy = pltpu.make_async_copy(s_hbm, sbuf, ssem)
    scopy.start()
    for s in range(4):
        chunk_copy(s).start()

    barrier = pltpu.get_barrier_semaphore()
    pl.semaphore_signal(barrier, inc=1, device_id=sibling, device_id_type=MESH)
    for dx, dy in AROUND:
        pl.semaphore_signal(barrier, inc=1, device_id=peer(chip_at(dx, dy)), device_id_type=MESH)
    for step in (1, 2):
        pl.semaphore_signal(barrier, inc=1, device_id=along_z(step), device_id_type=MESH)

    scopy.wait()
    sh[...], sl[...] = split(sbuf[...])

    def cores_copy(s):
        return remote(part.at[s, :, 1 - core], xbuf.at[s], xs_sem.at[s], xr_sem.at[s], sibling)

    def shard_copy(s, yy, q):
        return remote(outbuf.at[s, yy], rbuf.at[chip], rs_sem.at[q], rr_sem.at[chip], peer(q))

    @pl.loop(0, 5)
    def _(s):
        @pl.when(s < 4)
        def _():
            chunk_copy(s).wait()
            p = dot3(split(fbuf[lax.rem(x + far_first(s), 4)]), (sh[...], sl[...]))
            part[s] = p.reshape(4, 2, 32, 256)

            @pl.when(s == 0)
            def _():
                pl.semaphore_wait(barrier, 18)

            cores_copy(s).start()

        @pl.when(s > 0)
        def _():
            t = s - 1
            xt = lax.rem(x + far_first(t), 4)
            cores_copy(t).wait_recv()
            outbuf[t] = part[t, :, core] + xbuf[t]

            @pl.loop(0, 4)
            def _(u):
                yy = lax.rem(y + far_first(u), 4)
                q = xt * 4 + yy

                @pl.when(q != chip)
                def _():
                    shard_copy(t, yy, q).start()

    acc[...] = outbuf[3, y]
    for dx, dy in BY_SOURCE:
        q = chip_at(dx, dy)
        remote(outbuf.at[0, 0], rbuf.at[q], rs_sem.at[q], rr_sem.at[q], peer(q)).wait_recv()
        acc[...] += rbuf[q]

    chain[...] = acc[...]
    for h in range(2):
        samples[h, me] = acc[:, 128 * h:128 * h + 128]

    def own_copy(h, q):
        return remote(samples.at[h, me], samples.at[h, me], as_sem.at[h, q], ar_sem.at[h, chip], peer(q))

    def relay_copy(h, q):
        return remote(samples.at[h, q * 2 + core], samples.at[h, q * 2 + core], ws_sem.at[h, q], wr_sem.at[h, q], sibling)

    for h in range(2):
        for dx, dy in AROUND:
            own_copy(h, chip_at(dx, dy)).start()
        relay_copy(h, chip).start()

    def relay_half(h):
        for dx, dy in AROUND[::-1]:
            q = chip_at(dx, dy)
            remote(samples.at[h, me], samples.at[h, q * 2 + core], as_sem.at[h, q], ar_sem.at[h, q], peer(q)).wait_recv()
            relay_copy(h, q).start()

    def half_arrived(h):
        @pl.loop(0, 16)
        def _(q):
            remote(samples.at[h, q * 2 + core], samples.at[h, q * 2 + 1 - core], ws_sem.at[h, q], wr_sem.at[h, q],
                   sibling).wait_recv()

    def half_samples(h):
        return split(samples[h].reshape(1024, 128))

    def rows_of(piece, c):
        if piece == 0:
            return pl.ds(pl.multiple_of(c * 64, 64), 64)
        return pl.ds(pl.multiple_of(128 + c * 128, 128), 128)

    def z_copy(level, piece):
        at = rows_of(piece, core)
        i = level * 2 + piece
        return remote(hown.at[level, at], hother.at[level, at], zs_sem.at[i], zr_sem.at[i], along_z(level + 1))

    def z_direct():
        at = pl.ds(0, 128)
        return remote(hown.at[0, at], hother.at[0, at], zs_sem.at[0], zr_sem.at[0], along_z(1))

    def z_relay(level, piece, c):
        at = rows_of(piece, c)
        i = level * 2 + piece
        return remote(hother.at[level, at], hother.at[level, at], vs_sem.at[i], vr_sem.at[i], sibling)

    relay_half(0)
    half_arrived(0)
    first = half_samples(0)
    pair[0] = dot3(first, first, TN)

    def coupling_tile(i):
        cols = pl.ds(pl.multiple_of(i * 256, 256), 256)
        f = fbuf[:, :, cols].reshape(1024, 256)
        coupling[:, cols] = dot3((bth[...], btl[...]), split(f))

    @pl.loop(0, 3)
    def _(level):
        rank = ranks[level, z]
        zb[...] = masked(pair[0], rank, 0, 0)

        def between(s):
            if s == 1:
                @pl.when(level == 0)
                def _():
                    relay_half(1)

                @pl.when(level > 0)
                def _():
                    z_copy(level - 1, 1).wait_recv()
                    z_relay(level - 1, 1, core).start()

        chol_inverse(zb, between)
        w11_out[...] = lower(zb[...])

        @pl.when(level == 0)
        def _():
            half_arrived(1)
            left, right = half_samples(0), half_samples(1)
            pair[1] = dot3(right, left, TN)
            pair[2] = dot3(right, right, TN)

        @pl.when(level > 0)
        def _():
            z_relay(level - 1, 1, 1 - core).wait_recv()
            pair[1] += hother[level - 1, 128:256]
            pair[2] += hother[level - 1, 256:384]
            z_copy(level - 1, 1).wait_send()
            z_relay(level - 1, 1, core).wait_send()

        @pl.when(level < 2)
        def _():
            w11 = w11_out[...]
            m21 = schur(zb, split(w11), masked(pair[1], rank, 128, 0), masked(pair[2], rank, 128, 128))
            gb[:128, :128] = pair[0]
            gb[:128, 128:] = pair[1].T
            gb[128:, :128] = pair[1]
            gb[128:, 128:] = pair[2]
            g = gb[...]
            gr = row_masked(g, rank)
            gc = col_masked(g, rank)
            w1, m2 = split(w11), split(m21)
            gr1, gc1 = split(gr[:128]), split(gc[:, :128])
            c1 = split(dot3(w1, gr1))
            ct1 = split(dot3(gc1, w1, NT))
            r2 = split(gr[128:] + dot3(m2, gr1))
            rt2 = split(gc[:, 128:] + dot3(gc1, m2, NT))
            hb[...] = dot3(ct1, c1)
            chol_inverse(zb, nothing)
            w22 = lower(zb[...])
            w2 = split(w22)
            c2 = split(dot3(w2, r2))
            ct2 = split(dot3(rt2, w2, NT))

            def block(i, j):
                a, b = slice(128 * i, 128 * i + 128), slice(128 * j, 128 * j + 128)
                return hb[a, b] + dot3((ct2[0][a], ct2[1][a]), (c2[0][:, b], c2[1][:, b]))

            h11 = block(0, 0)
            hown[level, 0:128] = h11

            @pl.when(level == 0)
            def _():
                z_direct().start()

            @pl.when(level == 1)
            def _():
                z_copy(1, 0).start()

            h21, h22 = block(1, 0), block(1, 1)
            hown[level, 128:256] = h21
            hown[level, 256:384] = h22
            z_copy(level, 1).start()
            pair[0] = h11
            pair[1] = h21
            pair[2] = h22
            for i in range(2):
                cb[i, :128] = c1[i]
                cb[i, 128:] = c2[i]
            wb[:128, :128] = w11
            wb[:128, 128:] = jnp.zeros((128, 128), F32)
            wb[128:, :128] = dot3(w2, m2)
            wb[128:, 128:] = w22
            chain[...] = dot3(split(col_masked(chain[...], rank)), split(wb[...]), NT)

            @pl.when(level == 0)
            def _():
                leaf[...] = chain[...]
                w0 = split(wb[...])
                whole = col_masked(jnp.concatenate([samples[0].reshape(1024, 128), samples[1].reshape(1024, 128)], axis=1), rank)
                bth[...], btl[...] = split(dot3(w0, split(whole), NT))

            @pl.loop(0, 2)
            def _(i):
                coupling_tile(level * 2 + i)

            @pl.when(level == 1)
            def _():
                @pl.loop(4, 6)
                def _(i):
                    coupling_tile(i)

            chain[...] = dot3(split(chain[...]), (cb[0], cb[1]))

            @pl.when(level == 0)
            def _():
                z_direct().wait()

            @pl.when(level == 1)
            def _():
                z_copy(1, 0).wait()
                relay = z_relay(1, 0, core)
                relay.start()

                @pl.loop(6, 8)
                def _(i):
                    coupling_tile(i)

                z_relay(1, 0, 1 - core).wait_recv()
                relay.wait_send()

            pair[0] += hother[level, 0:128]

    for s in range(4):
        cores_copy(s).wait_send()
    for dx, dy in AROUND:
        q = chip_at(dx, dy)
        shard_copy(0, 0, q).wait_send()
        own_copy(0, q).wait_send()
        own_copy(1, q).wait_send()

    @pl.loop(0, 16)
    def _(q):
        relay_copy(0, q).wait_send()
        relay_copy(1, q).wait_send()


def last_kernel(ranks, leaf_in, coupling_in, w11, pair, chain, leaf, top, coupling, zb, sem):
    copies = [pltpu.make_async_copy(coupling_in, coupling, sem.at[0]), pltpu.make_async_copy(leaf_in, leaf, sem.at[1])]
    for copy in copies:
        copy.start()
    rank = ranks[2, lax.axis_index("row")]
    w = split(w11[...])
    m21 = split(schur(zb, w, masked(pair[1], rank, 128, 0), masked(pair[2], rank, 128, 128)))
    t = col_masked(chain[...], rank)
    left = split(t[:, :128])
    right = t[:, 128:] + dot3(left, m21, NT)
    chol_inverse(zb, nothing)
    top[:, :128] = dot3(left, w, NT)
    top[:, 128:] = dot3(split(right), split(lower(zb[...])), NT)
    for copy in copies:
        copy.wait()


def body(frontal, sketch, rank_table):
    vmem = pl.BlockSpec(memory_space=pltpu.VMEM)
    hbm = pl.BlockSpec(memory_space=pltpu.HBM)
    dma = pltpu.SemaphoreType.DMA
    bf16 = jnp.bfloat16
    smem = pl.BlockSpec(memory_space=pltpu.SMEM)
    frontal = pltpu.with_memory_space_constraint(frontal, pltpu.HBM)
    sketch = pltpu.with_memory_space_constraint(sketch, pltpu.HBM)
    rank_table = pltpu.with_memory_space_constraint(rank_table, pltpu.HBM)
    held = pl.pallas_call(
        kernel,
        out_shape=(pltpu.VMEM((32, 256), F32), pltpu.VMEM((256, 2048), F32), pltpu.VMEM((128, 128), F32),
                   pltpu.VMEM((3, 128, 128), F32), pltpu.VMEM((32, 256), F32)),
        in_specs=[smem, hbm, hbm],
        out_specs=(vmem,) * 5,
        scratch_shapes=[
            pltpu.VMEM((4, 256, 2048), F32),
            pltpu.VMEM((2048, 256), F32),
            pltpu.VMEM((2048, 256), bf16),
            pltpu.VMEM((2048, 256), bf16),
            pltpu.VMEM((4, 4, 2, 32, 256), F32),
            pltpu.VMEM((4, 4, 32, 256), F32),
            pltpu.VMEM((4, 4, 32, 256), F32),
            pltpu.VMEM((16, 32, 256), F32),
            pltpu.VMEM((32, 256), F32),
            pltpu.VMEM((2, 32, 32, 128), F32),
            pltpu.VMEM((128, 128), F32),
            pltpu.VMEM((256, 256), F32),
            pltpu.VMEM((256, 256), F32),
            pltpu.VMEM((256, 256), F32),
            pltpu.VMEM((2, 256, 256), bf16),
            pltpu.VMEM((256, 1024), bf16),
            pltpu.VMEM((256, 1024), bf16),
            pltpu.VMEM((2, 384, 128), F32),
            pltpu.VMEM((2, 384, 128), F32),
            dma((4,)), dma, dma((4,)), dma((4,)),
            dma((16,)), dma((16,)), dma((2, 16)), dma((2, 16)), dma((2, 16)), dma((2, 16)),
            dma((4,)), dma((4,)), dma((4,)), dma((4,)),
        ],
        compiler_params=pltpu.CompilerParams(collective_id=0, has_side_effects=True, vmem_limit_bytes=40 * 2**20),
        cost_estimate=pl.CostEstimate(flops=7 * 2**30, bytes_accessed=12 * 2**20, transcendentals=0),
    )(rank_table, frontal, sketch)
    return pl.pallas_call(
        last_kernel,
        out_shape=(jax.ShapeDtypeStruct((32, 256), F32), jax.ShapeDtypeStruct((32, 256), F32),
                   jax.ShapeDtypeStruct((256, 2048), F32)),
        in_specs=[smem] + [vmem] * 5,
        out_specs=(hbm, vmem, hbm),
        scratch_shapes=[pltpu.VMEM((128, 128), F32), dma((2,))],
        compiler_params=pltpu.CompilerParams(vmem_limit_bytes=16 * 2**20),
    )(rank_table, *held)


def solution(mesh):
    return jax.shard_map(
        body,
        mesh=mesh,
        in_specs=(P("row", "col"), P("col", None), P()),
        out_specs=(P(("row", "col"), None), P(("row", "col"), None), P("row", "col")),
        check_vma=False,
    )
```
